256 devices in a mesh: section: 4 (over y_lo, core), tensor: 8 (over z), dp: 8 (over y_hi, x).
Axes of the slice: x: 4, y: 4 (y_hi: 2, y_lo: 2; y = y_hi * 2 + y_lo), z: 8, core: 2. Of those that a mesh axis runs over, the one named last changes fastest.
Arguments:
- x_in: bfloat16 [1, 1024, 2048], P(None, 'dp', ('section', 'tensor')), may hold values from -40 to 40
- gate_weight: bfloat16 [4, 2048, 7168], P('section', None, 'tensor'), may hold values from -0.125 to 0.125
- up_weight: bfloat16 [4, 2048, 7168], P('section', None, 'tensor'), may hold values from -0.125 to 0.125
- down_weight: bfloat16 [4, 7168, 2048], P('section', 'tensor'), may hold values from -0.0625 to 0.0625
- norm_gain: float32 [4, 2048], P('section'), may hold values from 0.1 to 1.9
- cotangent: bfloat16 [1, 1024, 2048], P(None, 'dp', ('section', 'tensor')), may hold values from -0.5 to 0.5
Outputs:
- new_grad: float32 [4, 7168, 2048], P('section', 'tensor', 'dp')
The draws below stay inside these ranges and needn't reach their ends.
All inputs are finite; a program needn't handle non-finite values.
Results may differ from the reference program's by a relative error of at most 0.035.
Values may be sent and summed in bfloat16 or wider, within the bound.
A program may use at most 128 MiB of HBM per device.

```python
import jax
import jax.numpy as jnp
from jax import lax

D = 2048
FF = 7168
MICRO = 1
BATCH = 1024
N_SECTION = 4
N_TENSOR = 8


def draw_x_in(key, part):
    key = jax.random.fold_in(key, 11)
    subkeys = jax.random.split(key, 3)
    array_shape = (MICRO, BATCH, D)
    column_draw = jax.random.uniform(subkeys[1], (1, 1, D), jnp.float32, 0.0, 1.0)
    row_draw = jax.random.uniform(subkeys[2], (MICRO, BATCH, 1), jnp.float32, 0.0, 1.0)
    column_scale = 10.0 ** (column_draw - 0.5)
    row_scale = 10.0 ** (row_draw - 0.5)
    base_draw = jnp.clip(jax.random.normal(subkeys[0], array_shape, jnp.float32), -4.0, 4.0)
    return (base_draw * row_scale * column_scale).astype(jnp.bfloat16)


def levels(rng, extent, shards, smallest, top_value):
    loudness, own = 1.0, jax.random.fold_in(rng, 6)
    for position, blocks in shards:
        steps = jnp.exp(jax.random.uniform(jax.random.fold_in(own, position), (blocks,), jnp.float32, smallest / len(shards), top_value / len(shards)))
        loudness = loudness * jnp.repeat(steps, extent[position] // blocks).reshape([-1 if axis == position else 1 for axis in range(len(extent))])
    return loudness


def centred(key, dims, width, bound, pieces=(), kind=jnp.bfloat16):
    values = jax.random.normal(key, dims, jnp.float32) * width
    if len(pieces) > 0:
        values = levels(key, dims, pieces, -0.22, 0.18) * values
    return jnp.clip(values, min=-bound, max=bound).astype(kind)


def setup_inputs(seed: int = 0) -> dict:
    keys = jax.random.split(jax.random.key(seed), 7)
    x_in = draw_x_in(jax.random.fold_in(keys[6], 71), 0)
    gate_weight = centred(keys[1], (N_SECTION, D, FF), D ** -0.5, 0.125, ((0, 4), (2, 8)))
    up_weight = centred(keys[2], (N_SECTION, D, FF), D ** -0.5, 0.125, ((0, 4), (2, 8)))
    down_weight = centred(keys[3], (N_SECTION, FF, D), FF ** -0.5, 0.0625, ((0, 4), (1, 8)))
    norm_gain = jnp.clip(1.0 + 0.18 * jax.random.normal(keys[4], (N_SECTION, D), jnp.float32), 0.1, 1.9)
    cotangent = centred(keys[5], (MICRO, BATCH, D), (1.0 / (MICRO * BATCH) ** 0.5), 0.5, ((1, 8), (2, 32)))
    return {"x_in": x_in, "gate_weight": gate_weight, "up_weight": up_weight, "down_weight": down_weight, "norm_gain": norm_gain, "cotangent": cotangent}


EPSILON = 1e-05

def normalize(activations, norm_scale):
    values = activations.astype(jnp.float32)
    inv_rms = lax.rsqrt(lax.optimization_barrier(jnp.mean(values * values, axis=-1, keepdims=True)) + EPSILON)
    return (values * inv_rms * norm_scale).astype(jnp.bfloat16)

def norm_back(activations, norm_scale, incoming):
    values = activations.astype(jnp.float32)
    inv_rms = lax.rsqrt(lax.optimization_barrier(jnp.mean(values * values, axis=-1, keepdims=True)) + EPSILON)
    weighted = incoming * norm_scale
    return inv_rms * weighted - values * inv_rms * inv_rms * inv_rms * lax.optimization_barrier(jnp.mean(values * weighted, axis=-1, keepdims=True))

def rounded_blocks(term_pairs, blocks):
    summed = None
    for block_index in range(blocks):
        block_sum = None
        for left_op, right_op in term_pairs:
            block_width = left_op.shape[1] // blocks
            low = block_index * block_width
            product = jnp.dot(left_op[:, low:low + block_width], right_op[low:low + block_width], preferred_element_type=jnp.float32)
            block_sum = product if block_sum is None else block_sum + product
        block_sum = lax.optimization_barrier(block_sum.astype(jnp.bfloat16)).astype(jnp.float32)
        summed = block_sum if summed is None else summed + block_sum
    return summed

def reference(x_in, gate_weight, up_weight, down_weight, norm_gain, cotangent):
    gradients = [jnp.zeros((FF, D), jnp.float32) for layer_index in range(N_SECTION)]
    for micro_index in range(MICRO):
        current = x_in[micro_index]
        inputs = []
        expanded_list = []
        for layer_index in range(N_SECTION):
            inputs.append(current)
            normed = normalize(current, norm_gain[layer_index])
            gate_pre = jnp.dot(normed, gate_weight[layer_index], preferred_element_type=jnp.float32)
            up_pre = jnp.dot(normed, up_weight[layer_index], preferred_element_type=jnp.float32)
            hidden = (jax.nn.silu(gate_pre) * up_pre).astype(jnp.bfloat16)
            branch = rounded_blocks([(hidden, down_weight[layer_index])], N_TENSOR)
            current = (current.astype(jnp.float32) + branch).astype(jnp.bfloat16)
            renormed = normalize(current, norm_gain[layer_index])
            gate_new = jnp.dot(renormed, gate_weight[layer_index], preferred_element_type=jnp.float32)
            up_new = jnp.dot(renormed, up_weight[layer_index], preferred_element_type=jnp.float32)
            expanded_list.append((jax.nn.silu(gate_new) * up_new).astype(jnp.bfloat16))
        incoming = cotangent[micro_index]
        for layer_index in reversed(range(N_SECTION)):
            gradients[layer_index] = gradients[layer_index] + jnp.dot(expanded_list[layer_index].T, incoming, preferred_element_type=jnp.float32)
            if layer_index > 0:
                normed = normalize(inputs[layer_index], norm_gain[layer_index])
                gate_pre = jnp.dot(normed, gate_weight[layer_index], preferred_element_type=jnp.float32)
                up_pre = jnp.dot(normed, up_weight[layer_index], preferred_element_type=jnp.float32)
                back_hidden = jnp.dot(incoming, down_weight[layer_index].T, preferred_element_type=jnp.float32)
                sigmoid_gate = jax.nn.sigmoid(gate_pre)
                d_up = (back_hidden * gate_pre * sigmoid_gate).astype(jnp.bfloat16)
                d_gate = (back_hidden * up_pre * sigmoid_gate * (1.0 + gate_pre * (1.0 - sigmoid_gate))).astype(jnp.bfloat16)
                normed_grad = rounded_blocks([(d_gate, gate_weight[layer_index].T), (d_up, up_weight[layer_index].T)], N_TENSOR)
                change = norm_back(inputs[layer_index], norm_gain[layer_index], normed_grad)
                incoming = (incoming.astype(jnp.float32) + change).astype(jnp.bfloat16)
    return jnp.stack(gradients)
```

```python
import functools

import jax
import jax.numpy as jnp
from jax import lax
from jax.experimental import pallas as pl
from jax.experimental.pallas import tpu as pltpu
from jax.sharding import PartitionSpec as P

EPSILON = 1e-05
F32, BF16 = jnp.float32, jnp.bfloat16
CONTRACT_FIRST = (((0,), (0,)), ((), ()))
STREAMS = 2
PIECE = 64


def dot(left, right):
    return jnp.dot(left, right, preferred_element_type=F32)


def chunked(rows):
    half = rows.shape[1] // 2
    return jnp.concatenate([rows[:, :half], rows[:, half:]], axis=0)


def inv_rms(low, high, features):
    square = jnp.sum(low * low, axis=-1, keepdims=True) + jnp.sum(high * high, axis=-1, keepdims=True)
    return lax.rsqrt(square / features + EPSILON)


def kernel(
    sizes, x_ref, c_ref, gain_ref, gate_hbm, up_hbm, down_hbm, out_ref,
    gate, up, down, down_t, gate_up_t, pieces, landing, hc, hn, qc, normed, product, hidden, slopes,
    gate_factor, up_factor, back_hidden, f_out, f_in, b_out, b_in, f_sum, b_sum, tail_out, tail_mid,
    tail_in, q_rows, q_cols, expanded,
    w_sem, piece_send, piece_recv, fs_send, fs_recv, bs_send, bs_recv, fg_send, fg_recv, bg_send, bg_recv,
    back_send, back_recv, own_send, own_recv, e_send, e_recv, q_send, q_recv, t1_send, t1_recv, t2_send,
    t2_recv, go,
):
    sections, tensors, replicas = sizes
    s, t, r = lax.axis_index("section"), lax.axis_index("tensor"), lax.axis_index("dp")
    last = sections - 1
    features = down.shape[1]
    half = features // 2
    units = gate.shape[1]
    rows = normed.shape[0]
    offsets = sorted(range(1, tensors), key=lambda d: (-min(d, tensors - d), d))
    me = s * tensors + t

    def remote(src, dst, send, recv, **where):
        return pltpu.make_async_remote_copy(
            src_ref=src, dst_ref=dst, send_sem=send, recv_sem=recv, device_id=where,
            device_id_type=pl.DeviceIdType.MESH,
        )

    def other(d):
        return lax.rem(t + d, tensors)

    def replica(d):
        return lax.rem(r + d, replicas)

    loads = [
        pltpu.make_async_copy(src.at[0], dst, w_sem.at[i])
        for i, (src, dst) in enumerate(((gate_hbm, gate), (up_hbm, up), (down_hbm, down)))
    ]
    for load in loads:
        load.start()

    barrier = pltpu.get_barrier_semaphore()
    for d in range(1, sections * tensors):
        to = lax.rem(me + d, sections * tensors)
        pl.semaphore_signal(
            barrier, inc=1, device_id={"section": to // tensors, "tensor": lax.rem(to, tensors)},
            device_id_type=pl.DeviceIdType.MESH,
        )
    for d in range(1, replicas):
        pl.semaphore_signal(
            barrier, inc=1, device_id={"dp": replica(d)}, device_id_type=pl.DeviceIdType.MESH
        )
    for which, ref in enumerate((x_ref, c_ref)):
        for a in range(STREAMS):
            block = ref[0, a * rows:(a + 1) * rows, :].astype(F32)
            pieces[which, a] = jnp.concatenate(
                [block[:rows // 2], block[rows // 2:]], axis=1
            ).astype(BF16)
    pl.semaphore_wait(barrier, sections * tensors + replicas - 2)

    def piece_copy(which, a, d):
        return remote(
            pieces.at[which, a], landing.at[a, me], piece_send.at[which, a, d], piece_recv.at[a, me],
            section=0 if which == 0 else last, tensor=other(d),
        )

    def each_piece(action):
        for which, home in ((0, 0), (1, last)):
            for a in range(STREAMS):
                for d in offsets:
                    action(piece_copy(which, a, d))

                @pl.when(s != home)
                def _():
                    action(piece_copy(which, a, 0))

    each_piece(lambda copy: copy.start())

    def gather_pieces(which, a, dst):
        landing[a, me] = pieces[which, a]

        @pl.loop(1, sections * tensors)
        def _(d):
            src = lax.rem(me + d, sections * tensors)
            remote(
                pieces.at[which, a], landing.at[a, src], piece_send.at[which, a, 0], piece_recv.at[a, src],
                tensor=other(1),
            ).wait_recv()

        left = lax.broadcasted_iota(jnp.int32, (rows // 2, 2 * PIECE), 1) < PIECE

        def block(j):
            first, second = landing[a, 2 * j].astype(F32), landing[a, 2 * j + 1].astype(F32)
            top = jnp.where(left, first, pltpu.roll(second, PIECE, 1))
            bottom = jnp.where(left, pltpu.roll(first, PIECE, 1), second)
            return jnp.concatenate([top, bottom], axis=0)

        for j in range(half // 128):
            low, high = block(j), block(j + half // 128)
            for o in range(tensors):
                part = slice(8 * o, 8 * o + 8)
                dst[a, o, :, 128 * j:128 * j + 128] = jnp.concatenate(
                    [low[part], high[part]], axis=0
                ).astype(BF16)

    def wait_chunks(buffer, send, recv, a):
        for d in reversed(offsets):
            src = other(d)
            remote(buffer.at[a, src], buffer.at[a, src], send.at[a, 0], recv.at[a, src], tensor=other(1)).wait_recv()

    def halves(chunk):
        return chunk[:8], chunk[8:]

    def normalize(buffer, a):
        gain = gain_ref[...]
        for k in range(tensors // 2):
            pair = []
            for o in (2 * k, 2 * k + 1):
                low, high = halves(buffer[a, o].astype(F32))
                scale = inv_rms(low, high, features)
                pair.append(
                    jnp.concatenate([low * scale * gain[:, :half], high * scale * gain[:, half:]], axis=1)
                )
            normed[16 * k:16 * k + 16, :] = jnp.concatenate(pair, axis=0).astype(BF16)

    def fill_q_rows(a):
        for k in range(tensors // 2):
            pair = [
                jnp.concatenate(halves(qc[a, o].astype(F32)), axis=1) for o in (2 * k, 2 * k + 1)
            ]
            q_rows[a, 16 * k:16 * k + 16, :] = jnp.concatenate(pair, axis=0).astype(BF16)

    def scatter(out, land, send, recv, a):
        for o in range(tensors):
            out[a, o] = chunked(product[8 * o:8 * o + 8, :]).astype(BF16)
        for d in offsets:
            remote(out.at[a, other(d)], land.at[a, t], send.at[a, d], recv.at[a, t], tensor=other(d)).start()

    def scatter_sent(out, land, send, recv, a):
        for d in offsets:
            remote(out.at[a, other(d)], land.at[a, t], send.at[a, d], recv.at[a, t], tensor=other(d)).wait_send()

    def summed(out, land, send, recv, a):
        total = out[a, t].astype(F32)
        for d in reversed(offsets):
            src = other(d)
            remote(land.at[a, src], land.at[a, src], send.at[a, 0], recv.at[a, src], tensor=other(1)).wait_recv()
            total = total + land[a, src].astype(F32)
        return total

    def spread(src, dst, send, recv, a, section):
        return [
            remote(src.at[a], dst.at[a, t], send.at[a, d], recv.at[a, t], section=section, tensor=other(d))
            for d in (*offsets, 0)
        ]

    def own_spread(a):
        return [
            remote(f_sum.at[a], hn.at[a, t], own_send.at[a, d], own_recv.at[a, t], tensor=other(d))
            for d in offsets
        ]

    def send_back(a):
        return remote(
            hc.at[a], hn.at[a], back_send.at[a], back_recv.at[a], section=jnp.maximum(s - 1, 0), tensor=t
        )

    def e_copy(d):
        return remote(expanded.at[r], expanded.at[r], e_send.at[d], e_recv.at[r], dp=replica(d))

    def q_copy(d):
        width = q_cols.shape[-1]
        columns = pl.ds(pl.multiple_of(replica(d) * width, width), width)
        return remote(q_rows.at[:, :, columns], q_cols.at[r], q_send.at[d], q_recv.at[r], dp=replica(d))

    def send_q():
        width = q_cols.shape[-1]
        for d in range(1, replicas):
            q_copy(d).start()
        q_cols[r] = q_rows[:, :, pl.ds(pl.multiple_of(r * width, width), width)]

    def tail_copy(a, d):
        return remote(
            tail_out.at[a, replica(d)], tail_mid.at[a, r], t1_send.at[a, d], t1_recv.at[a, r], dp=replica(d)
        )

    def owner_forward(a):
        total = summed(f_out, f_in, fs_send, fs_recv, a)
        f_sum[a] = (hc[a, t].astype(F32) + total).astype(BF16)

    def owner_backward(a):
        grad_low, grad_high = halves(summed(b_out, b_in, bs_send, bs_recv, a))
        low, high = halves(hc[a, t].astype(F32))
        q_low, q_high = halves(qc[a, t].astype(F32))
        gain = gain_ref[...]
        scale = inv_rms(low, high, features)
        w_low, w_high = grad_low * gain[:, :half], grad_high * gain[:, half:]
        mean = (
            jnp.sum(low * w_low, axis=-1, keepdims=True) + jnp.sum(high * w_high, axis=-1, keepdims=True)
        ) / features
        pull = scale * scale * scale * mean
        q_low = q_low + scale * w_low - low * pull
        q_high = q_high + scale * w_high - high * pull
        return q_low, q_high

    def backward_product(a, incoming):
        slopes[:, :units] = (incoming * gate_factor[a]).astype(BF16)
        slopes[:, units:] = (incoming * up_factor[a]).astype(BF16)
        product[...] = dot(slopes[...], gate_up_t[...])
        scatter(b_out, b_in, bs_send, bs_recv, a)

    def pass_back(a):
        q_low, q_high = owner_backward(a)
        b_sum[a] = jnp.concatenate([q_low, q_high], axis=0).astype(BF16)
        for copy in spread(b_sum, qc, bg_send, bg_recv, a, jnp.maximum(s - 1, 0)):
            copy.start()

    def expand(a):
        normalize(hn, a)
        gate_new = dot(normed[...], gate[...])
        up_new = dot(normed[...], up[...])
        expanded[r, a] = (gate_new / (1.0 + jnp.exp(-gate_new)) * up_new).astype(BF16)

    for load in loads:
        load.wait()

    @pl.when(s > 0)
    def _():
        @pl.loop(0, features // 256)
        def _(j):
            part = pl.ds(pl.multiple_of(256 * j, 256), 256)
            down_t[part, :] = down[:, part].T
            gate_up_t[:units, part] = gate[part, :].T
            gate_up_t[units:, part] = up[part, :].T

    @pl.when(s == last)
    def _():
        @pl.loop(0, STREAMS)
        def _(a):
            gather_pieces(1, a, qc)
            fill_q_rows(a)
            back_hidden[a] = dot(q_rows[a], down_t[...])

        send_q()

    @pl.loop(0, STREAMS)
    def _(a):
        @pl.when(s == 0)
        def _():
            gather_pieces(0, a, hc)

        @pl.when(s > 0)
        def _():
            wait_chunks(hc, fg_send, fg_recv, a)
            remote(hc.at[a, t], hc.at[a, t], fg_send.at[a, 0], fg_recv.at[a, t], tensor=other(1)).wait_recv()
            send_back(a).start()

        normalize(hc, a)
        gate_pre = dot(normed[...], gate[...])
        up_pre = dot(normed[...], up[...])
        sigmoid = 1.0 / (1.0 + jnp.exp(-gate_pre))
        silu = gate_pre * sigmoid
        hidden[a] = (silu * up_pre).astype(BF16)
        up_factor[a] = silu
        gate_factor[a] = up_pre * sigmoid * (1.0 + gate_pre * (1.0 - sigmoid))

        @pl.when(s < last)
        def _():
            product[...] = dot(hidden[a], down[...])
            scatter(f_out, f_in, fs_send, fs_recv, a)

        @pl.when(s == last)
        def _():
            backward_product(a, back_hidden[a])

    @pl.when(s < last)
    def _():
        @pl.loop(0, STREAMS)
        def _(a):
            owner_forward(a)
            for copy in spread(f_sum, hc, fg_send, fg_recv, a, jnp.minimum(s + 1, last)):
                copy.start()

        @pl.loop(0, STREAMS)
        def _(a):
            send_back(a).wait_recv()
            expand(a)

        for d in range(1, replicas):
            e_copy(d).start()

    @pl.when(jnp.logical_and(s > 0, s < last))
    def _():
        @pl.loop(0, STREAMS)
        def _(a):
            wait_chunks(qc, bg_send, bg_recv, a)
            remote(qc.at[a, t], qc.at[a, t], bg_send.at[a, 0], bg_recv.at[a, t], tensor=other(1)).wait_recv()
            fill_q_rows(a)
            backward_product(a, dot(q_rows[a], down_t[...]))

    @pl.when(s > 1)
    def _():
        @pl.loop(0, STREAMS)
        def _(a):
            pass_back(a)

    @pl.when(s == last - 1)
    def _():
        pl.semaphore_signal(
            go, inc=1, device_id={"section": last, "tensor": t}, device_id_type=pl.DeviceIdType.MESH
        )

    @pl.when(s == 1)
    def _():
        @pl.loop(0, STREAMS)
        def _(a):
            sides = owner_backward(a)
            width = q_cols.shape[-1]
            for k in range(replicas):
                side = sides[(k * width) // half]
                at = (k * width) % half
                tail_out[a, k] = jnp.concatenate(
                    [side[:, at:at + 128], side[:, at + 128:at + 256]], axis=0
                ).astype(BF16)
            for d in range(1, replicas):
                tail_copy(a, d).start()
            tail_mid[a, r] = tail_out[a, r]

        @pl.loop(0, STREAMS)
        def _(a):
            for d in range(1, replicas):
                src = replica(d)
                remote(
                    tail_mid.at[a, src], tail_mid.at[a, src], t1_send.at[a, 0], t1_recv.at[a, src], dp=replica(1)
                ).wait_recv()
            for copy in spread(tail_mid, tail_in, t2_send, t2_recv, a, 0):
                copy.start()

    @pl.when(jnp.logical_and(s > 0, s < last))
    def _():
        send_q()

    @pl.when(s == last)
    def _():
        pl.semaphore_wait(go, 1)

        @pl.loop(0, STREAMS)
        def _(a):
            product[...] = dot(hidden[a], down[...])
            scatter(f_out, f_in, fs_send, fs_recv, a)

        @pl.loop(0, STREAMS)
        def _(a):
            owner_forward(a)
            hn[a, t] = f_sum[a]
            for copy in own_spread(a):
                copy.start()

        @pl.loop(0, STREAMS)
        def _(a):
            wait_chunks(hn, own_send, own_recv, a)
            expand(a)

        for d in range(1, replicas):
            e_copy(d).start()

    @pl.when(s > 0)
    def _():
        for d in range(1, replicas):
            src = replica(d)
            remote(q_cols.at[src], q_cols.at[src], q_send.at[0], q_recv.at[src], dp=replica(1)).wait_recv()

    for d in range(1, replicas):
        src = replica(d)
        remote(expanded.at[src], expanded.at[src], e_send.at[0], e_recv.at[src], dp=replica(1)).wait_recv()

    @pl.when(s == 0)
    def _():
        @pl.loop(0, STREAMS)
        def _(a):
            wait_chunks(tail_in, t2_send, t2_recv, a)
            remote(tail_in.at[a, t], tail_in.at[a, t], t2_send.at[a, 0], t2_recv.at[a, t], tensor=other(1)).wait_recv()
            for k in range(replicas):
                for pair in range(tensors // 2):
                    both = [
                        jnp.concatenate(halves(tail_in[a, o, k].astype(F32)), axis=1)
                        for o in (2 * pair, 2 * pair + 1)
                    ]
                    q_cols[k, a, 16 * pair:16 * pair + 16, :] = jnp.concatenate(both, axis=0).astype(BF16)

    every = replicas * STREAMS * rows
    out_ref[0] = lax.dot_general(
        expanded[...].reshape(every, units), q_cols[...].reshape(every, q_cols.shape[-1]),
        CONTRACT_FIRST, preferred_element_type=F32,
    )

    each_piece(lambda copy: copy.wait_send())
    for d in range(1, replicas):
        e_copy(d).wait_send()

    @pl.when(s > 0)
    def _():
        for d in range(1, replicas):
            q_copy(d).wait_send()

    @pl.loop(0, STREAMS)
    def _(a):
        scatter_sent(f_out, f_in, fs_send, fs_recv, a)

        @pl.when(s > 0)
        def _():
            send_back(a).wait_send()
            scatter_sent(b_out, b_in, bs_send, bs_recv, a)

        @pl.when(s < last)
        def _():
            for copy in spread(f_sum, hc, fg_send, fg_recv, a, jnp.minimum(s + 1, last)):
                copy.wait_send()

        @pl.when(s == last)
        def _():
            for copy in own_spread(a):
                copy.wait_send()

        @pl.when(s > 1)
        def _():
            for copy in spread(b_sum, qc, bg_send, bg_recv, a, jnp.maximum(s - 1, 0)):
                copy.wait_send()

        @pl.when(s == 1)
        def _():
            for d in range(1, replicas):
                tail_copy(a, d).wait_send()
            for copy in spread(tail_mid, tail_in, t2_send, t2_recv, a, 0):
                copy.wait_send()


def solution(mesh):
    sections, tensors, replicas = (mesh.shape[name] for name in ("section", "tensor", "dp"))

    def shards(x_in, gate_weight, up_weight, down_weight, norm_gain, cotangent):
        features, units = gate_weight.shape[1:]
        rows = 8 * tensors
        width = features // replicas
        half = features // 2
        vmem, dma = pltpu.VMEM, pltpu.SemaphoreType.DMA
        chunks = vmem((STREAMS, tensors, 16, half), BF16)
        chunk = vmem((STREAMS, 16, half), BF16)
        factor = vmem((STREAMS, rows, units), F32)
        pair = [dma((STREAMS, tensors)), dma((STREAMS, tensors))]
        local = pl.BlockSpec(memory_space=pltpu.VMEM)
        anywhere = pl.BlockSpec(memory_space=pl.ANY)
        return pl.pallas_call(
            functools.partial(kernel, (sections, tensors, replicas)),
            out_shape=jax.ShapeDtypeStruct((1, units, width), F32),
            in_specs=[local, local, local, anywhere, anywhere, anywhere],
            out_specs=local,
            scratch_shapes=[
                vmem((features, units), BF16),
                vmem((features, units), BF16),
                vmem((units, features), BF16),
                vmem((features, units), BF16),
                vmem((2 * units, features), BF16),
                vmem((2, STREAMS, rows // 2, 2 * PIECE), BF16),
                vmem((STREAMS, sections * tensors, rows // 2, 2 * PIECE), BF16),
                chunks, chunks, chunks,
                vmem((rows, features), BF16),
                vmem((rows, features), F32),
                vmem((STREAMS, rows, units), BF16),
                vmem((rows, 2 * units), BF16),
                factor, factor, factor,
                chunks, chunks, chunks, chunks,
                chunk, chunk,
                vmem((STREAMS, replicas, 16, width // 2), BF16),
                vmem((STREAMS, replicas, 16, width // 2), BF16),
                vmem((STREAMS, tensors, replicas, 16, width // 2), BF16),
                vmem((STREAMS, rows, features), BF16),
                vmem((replicas, STREAMS, rows, width), BF16),
                vmem((replicas, STREAMS, rows, units), BF16),
                dma((3,)),
                dma((2, STREAMS, tensors)), dma((STREAMS, sections * tensors)),
                *pair, *pair, *pair, *pair,
                dma((STREAMS,)), dma((STREAMS,)),
                *pair,
                dma((replicas,)), dma((replicas,)),
                dma((replicas,)), dma((replicas,)),
                dma((STREAMS, replicas)), dma((STREAMS, replicas)),
                *pair,
                pltpu.SemaphoreType.REGULAR,
            ],
            compiler_params=pltpu.CompilerParams(
                collective_id=0, has_side_effects=True, vmem_limit_bytes=56 * 1024 * 1024
            ),
            name="expanded_step",
        )(x_in, cotangent, norm_gain, gate_weight, up_weight, down_weight)

    placed = (
        P(None, "dp", ("section", "tensor")),
        P("section", None, "tensor"),
        P("section", None, "tensor"),
        P("section", "tensor", None),
        P("section", None),
        P(None, "dp", ("section", "tensor")),
    )
    return jax.shard_map(
        shards, mesh=mesh, in_specs=placed, out_specs=P("section", "tensor", "dp"), check_vma=False
    )
```

```python
import functools

import jax
import jax.numpy as jnp
from jax import lax
from jax.experimental import pallas as pl
from jax.experimental.pallas import tpu as pltpu
from jax.sharding import PartitionSpec as P

EPSILON = 1e-05
F32, BF16 = jnp.float32, jnp.bfloat16
CONTRACT_FIRST = (((0,), (0,)), ((), ()))
STREAMS = 2


def dot(left, right):
    return jnp.dot(left, right, preferred_element_type=F32)


def chunked(rows):
    half = rows.shape[1] // 2
    return jnp.concatenate([rows[:, :half], rows[:, half:]], axis=0)


def inv_rms(low, high, features):
    square = jnp.sum(low * low, axis=-1, keepdims=True) + jnp.sum(high * high, axis=-1, keepdims=True)
    return lax.rsqrt(square / features + EPSILON)


def kernel(
    sizes, x_ref, c_ref, gain_ref, gate_hbm, up_hbm, down_hbm, out_ref,
    gate_up, down, down_t, gate_up_t, landing, hc, hn, qc, normed, product, hidden, slopes,
    gate_factor, up_factor, back_hidden, f_out, f_in, b_out, b_in, f_sum, b_sum, tail_out, tail_mid,
    tail_in, q_rows, q_cols, expanded,
    w_sem, piece_send, piece_recv, fs_send, fs_recv, bs_send, bs_recv, fg_send, fg_recv, bg_send, bg_recv,
    back_send, back_recv, own_send, own_recv, e_send, e_recv, q_send, q_recv, t1_send, t1_recv, t2_send,
    t2_recv, go,
):
    sections, tensors, replicas = sizes
    s, t, r = lax.axis_index("section"), lax.axis_index("tensor"), lax.axis_index("dp")
    last = sections - 1
    features = down.shape[1]
    half = features // 2
    units = down.shape[0]
    rows = normed.shape[0]
    offsets = sorted(range(1, tensors), key=lambda d: (-min(d, tensors - d), d))
    me = s * tensors + t

    def remote(src, dst, send, recv, **where):
        return pltpu.make_async_remote_copy(
            src_ref=src, dst_ref=dst, send_sem=send, recv_sem=recv, device_id=where,
            device_id_type=pl.DeviceIdType.MESH,
        )

    def other(d):
        return lax.rem(t + d, tensors)

    def replica(d):
        return lax.rem(r + d, replicas)

    loads = [
        pltpu.make_async_copy(src.at[0], dst, w_sem.at[i])
        for i, (src, dst) in enumerate(
            ((gate_hbm, gate_up.at[:, :units]), (up_hbm, gate_up.at[:, units:]), (down_hbm, down))
        )
    ]
    for load in loads:
        load.start()

    barrier = pltpu.get_barrier_semaphore()
    for d in range(1, sections * tensors):
        to = lax.rem(me + d, sections * tensors)
        pl.semaphore_signal(
            barrier, inc=1, device_id={"section": to // tensors, "tensor": lax.rem(to, tensors)},
            device_id_type=pl.DeviceIdType.MESH,
        )
    for d in range(1, replicas):
        pl.semaphore_signal(
            barrier, inc=1, device_id={"dp": replica(d)}, device_id_type=pl.DeviceIdType.MESH
        )
    pl.semaphore_wait(barrier, sections * tensors + replicas - 2)

    inputs = (x_ref, c_ref)

    def piece_copy(which, d):
        return remote(
            inputs[which].at[0], landing.at[me], piece_send.at[which, d], piece_recv.at[me],
            section=0 if which == 0 else last, tensor=other(d),
        )

    def each_piece(action):
        for which, home in ((0, 0), (1, last)):
            for d in offsets:
                action(piece_copy(which, d))

            @pl.when(s != home)
            def _():
                action(piece_copy(which, 0))

    each_piece(lambda copy: copy.start())

    def gather_pieces(which, dst):
        landing[me] = inputs[which][0]

        @pl.loop(1, sections * tensors)
        def _(d):
            src = lax.rem(me + d, sections * tensors)
            remote(
                inputs[which].at[0], landing.at[src], piece_send.at[which, 0], piece_recv.at[src], tensor=other(1)
            ).wait_recv()

        def block(j):
            return jnp.concatenate([landing[2 * j].astype(F32), landing[2 * j + 1].astype(F32)], axis=0).T

        for j in range(half // 128):
            low, high = block(j), block(j + half // 128)
            for a in range(STREAMS):
                for o in range(tensors):
                    part = slice(a * rows + 8 * o, a * rows + 8 * o + 8)
                    dst[a, o, :, 128 * j:128 * j + 128] = jnp.concatenate(
                        [low[part], high[part]], axis=0
                    ).astype(BF16)

    def wait_chunks(buffer, send, recv, a):
        for d in reversed(offsets):
            src = other(d)
            remote(buffer.at[a, src], buffer.at[a, src], send.at[a, 0], recv.at[a, src], tensor=other(1)).wait_recv()

    def halves(chunk):
        return chunk[:8], chunk[8:]

    def normalize(buffer, a):
        gain = gain_ref[...]
        for k in range(tensors // 2):
            pair = []
            for o in (2 * k, 2 * k + 1):
                low, high = halves(buffer[a, o].astype(F32))
                scale = inv_rms(low, high, features)
                pair.append(
                    jnp.concatenate([low * scale * gain[:, :half], high * scale * gain[:, half:]], axis=1)
                )
            normed[16 * k:16 * k + 16, :] = jnp.concatenate(pair, axis=0).astype(BF16)

    def fill_q_rows(a):
        for k in range(tensors // 2):
            pair = [
                jnp.concatenate(halves(qc[a, o].astype(F32)), axis=1) for o in (2 * k, 2 * k + 1)
            ]
            q_rows[a, 16 * k:16 * k + 16, :] = jnp.concatenate(pair, axis=0).astype(BF16)

    def scatter(out, land, send, recv, a):
        for o in range(tensors):
            out[a, o] = chunked(product[8 * o:8 * o + 8, :]).astype(BF16)
        for d in offsets:
            remote(out.at[a, other(d)], land.at[a, t], send.at[a, d], recv.at[a, t], tensor=other(d)).start()

    def scatter_sent(out, land, send, recv, a):
        for d in offsets:
            remote(out.at[a, other(d)], land.at[a, t], send.at[a, d], recv.at[a, t], tensor=other(d)).wait_send()

    def summed(out, land, send, recv, a):
        total = out[a, t].astype(F32)
        for d in reversed(offsets):
            src = other(d)
            remote(land.at[a, src], land.at[a, src], send.at[a, 0], recv.at[a, src], tensor=other(1)).wait_recv()
            total = total + land[a, src].astype(F32)
        return total

    def spread(src, dst, send, recv, a, section):
        return [
            remote(src.at[a], dst.at[a, t], send.at[a, d], recv.at[a, t], section=section, tensor=other(d))
            for d in (*offsets, 0)
        ]

    def own_spread(a):
        return [
            remote(f_sum.at[a], hn.at[a, t], own_send.at[a, d], own_recv.at[a, t], tensor=other(d))
            for d in offsets
        ]

    def send_back(a):
        return remote(
            hc.at[a], hn.at[a], back_send.at[a], back_recv.at[a], section=jnp.maximum(s - 1, 0), tensor=t
        )

    across = replicas // 2
    partner = lax.rem(r + across, replicas)

    def along(d):
        return (r // across) * across + lax.rem(r + d, across)

    def e_copies(a):
        return [
            remote(expanded.at[r, a], expanded.at[r, a], e_send.at[a, d], e_recv.at[a, r], dp=to)
            for d, to in enumerate([partner] + [along(d) for d in range(1, across)])
        ]

    def e_passed(a):
        return [
            remote(
                expanded.at[partner, a], expanded.at[partner, a], e_send.at[a, across + d],
                e_recv.at[a, partner], dp=along(d),
            )
            for d in range(1, across)
        ]

    def e_wait(a, src):
        remote(expanded.at[src, a], expanded.at[src, a], e_send.at[a, 0], e_recv.at[a, src], dp=partner).wait_recv()

    def send_expanded(a):
        for copy in e_copies(a):
            copy.start()

    def pass_expanded():
        @pl.loop(0, STREAMS)
        def _(a):
            e_wait(a, partner)
            for copy in e_passed(a):
                copy.start()

    def q_copy(d):
        width = q_cols.shape[-1]
        columns = pl.ds(pl.multiple_of(replica(d) * width, width), width)
        return remote(q_rows.at[:, :, columns], q_cols.at[r], q_send.at[d], q_recv.at[r], dp=replica(d))

    def send_q():
        width = q_cols.shape[-1]
        for d in range(1, replicas):
            q_copy(d).start()
        q_cols[r] = q_rows[:, :, pl.ds(pl.multiple_of(r * width, width), width)]

    def tail_copy(a, d):
        return remote(
            tail_out.at[a, replica(d)], tail_mid.at[a, r], t1_send.at[a, d], t1_recv.at[a, r], dp=replica(d)
        )

    def owner_forward(a):
        total = summed(f_out, f_in, fs_send, fs_recv, a)
        f_sum[a] = (hc[a, t].astype(F32) + total).astype(BF16)

    def owner_backward(a):
        grad_low, grad_high = halves(summed(b_out, b_in, bs_send, bs_recv, a))
        low, high = halves(hc[a, t].astype(F32))
        q_low, q_high = halves(qc[a, t].astype(F32))
        gain = gain_ref[...]
        scale = inv_rms(low, high, features)
        w_low, w_high = grad_low * gain[:, :half], grad_high * gain[:, half:]
        mean = (
            jnp.sum(low * w_low, axis=-1, keepdims=True) + jnp.sum(high * w_high, axis=-1, keepdims=True)
        ) / features
        pull = scale * scale * scale * mean
        q_low = q_low + scale * w_low - low * pull
        q_high = q_high + scale * w_high - high * pull
        return q_low, q_high

    def backward_product(a, incoming):
        slopes[:, :units] = (incoming * gate_factor[a]).astype(BF16)
        slopes[:, units:] = (incoming * up_factor[a]).astype(BF16)
        product[...] = dot(slopes[...], gate_up_t[...])
        scatter(b_out, b_in, bs_send, bs_recv, a)

    def pass_back(a):
        q_low, q_high = owner_backward(a)
        b_sum[a] = jnp.concatenate([q_low, q_high], axis=0).astype(BF16)
        for copy in spread(b_sum, qc, bg_send, bg_recv, a, jnp.maximum(s - 1, 0)):
            copy.start()

    def expand(a):
        normalize(hn, a)
        both = dot(normed[...], gate_up[...])
        gate_new, up_new = both[:, :units], both[:, units:]
        expanded[r, a] = (gate_new / (1.0 + jnp.exp(-gate_new)) * up_new).astype(BF16)

    def allow(section):
        pl.semaphore_signal(
            go, inc=1, device_id={"section": section, "tensor": t}, device_id_type=pl.DeviceIdType.MESH
        )

    for load in loads:
        load.wait()

    @pl.when(s > 0)
    def _():
        @pl.loop(0, features // 256)
        def _(j):
            part = pl.ds(pl.multiple_of(256 * j, 256), 256)
            down_t[part, :] = down[:, part].T
            gate_up_t[:, part] = gate_up[part, :].T

    @pl.when(s == last)
    def _():
        gather_pieces(1, qc)

        @pl.loop(0, STREAMS)
        def _(a):
            fill_q_rows(a)
            back_hidden[a] = dot(q_rows[a], down_t[...])

        send_q()

    @pl.when(s == 0)
    def _():
        gather_pieces(0, hc)

    @pl.loop(0, STREAMS)
    def _(a):
        @pl.when(s > 0)
        def _():
            wait_chunks(hc, fg_send, fg_recv, a)
            remote(hc.at[a, t], hc.at[a, t], fg_send.at[a, 0], fg_recv.at[a, t], tensor=other(1)).wait_recv()
            send_back(a).start()

        normalize(hc, a)
        both = dot(normed[...], gate_up[...])
        gate_pre, up_pre = both[:, :units], both[:, units:]
        sigmoid = 1.0 / (1.0 + jnp.exp(-gate_pre))
        silu = gate_pre * sigmoid
        hidden[a] = (silu * up_pre).astype(BF16)
        up_factor[a] = silu
        gate_factor[a] = up_pre * sigmoid * (1.0 + gate_pre * (1.0 - sigmoid))

        @pl.when(s < last)
        def _():
            product[...] = dot(hidden[a], down[...])
            scatter(f_out, f_in, fs_send, fs_recv, a)

        @pl.when(s == last)
        def _():
            backward_product(a, back_hidden[a])

    @pl.when(s < last)
    def _():
        @pl.loop(0, STREAMS)
        def _(a):
            owner_forward(a)
            for copy in spread(f_sum, hc, fg_send, fg_recv, a, jnp.minimum(s + 1, last)):
                copy.start()

        @pl.loop(0, STREAMS)
        def _(a):
            send_back(a).wait_recv()

            @pl.when(jnp.logical_and(s == 1, a == STREAMS - 1))
            def _():
                allow(0)

            expand(a)

            @pl.when(s > 0)
            def _():
                send_expanded(a)

    @pl.when(s == 0)
    def _():
        pl.semaphore_wait(go, 1)

        @pl.loop(0, STREAMS)
        def _(a):
            send_expanded(a)

    @pl.when(s < 2)
    def _():
        pass_expanded()

    @pl.when(jnp.logical_and(s > 0, s < last))
    def _():
        @pl.loop(0, STREAMS)
        def _(a):
            wait_chunks(qc, bg_send, bg_recv, a)
            remote(qc.at[a, t], qc.at[a, t], bg_send.at[a, 0], bg_recv.at[a, t], tensor=other(1)).wait_recv()
            fill_q_rows(a)
            backward_product(a, dot(q_rows[a], down_t[...]))

    @pl.when(s > 1)
    def _():
        @pl.loop(0, STREAMS)
        def _(a):
            pass_back(a)

            @pl.when(jnp.logical_and(s == last - 1, a == 0))
            def _():
                allow(last)

    @pl.when(s == 2)
    def _():
        pass_expanded()

    @pl.when(s == 1)
    def _():
        @pl.loop(0, STREAMS)
        def _(a):
            sides = owner_backward(a)
            width = q_cols.shape[-1]
            for k in range(replicas):
                side = sides[(k * width) // half]
                at = (k * width) % half
                tail_out[a, k] = jnp.concatenate(
                    [side[:, at:at + 128], side[:, at + 128:at + 256]], axis=0
                ).astype(BF16)
            for d in range(1, replicas):
                tail_copy(a, d).start()
            tail_mid[a, r] = tail_out[a, r]

        @pl.loop(0, STREAMS)
        def _(a):
            for d in range(1, replicas):
                src = replica(d)
                remote(
                    tail_mid.at[a, src], tail_mid.at[a, src], t1_send.at[a, 0], t1_recv.at[a, src], dp=replica(1)
                ).wait_recv()
            for copy in spread(tail_mid, tail_in, t2_send, t2_recv, a, 0):
                copy.start()

    @pl.when(jnp.logical_and(s > 0, s < last))
    def _():
        send_q()

    @pl.when(s == last)
    def _():
        pl.semaphore_wait(go, 1)

        @pl.loop(0, STREAMS)
        def _(a):
            product[...] = dot(hidden[a], down[...])
            scatter(f_out, f_in, fs_send, fs_recv, a)

        @pl.loop(0, STREAMS)
        def _(a):
            owner_forward(a)
            hn[a, t] = f_sum[a]
            for copy in own_spread(a):
                copy.start()

        @pl.loop(0, STREAMS)
        def _(a):
            wait_chunks(hn, own_send, own_recv, a)
            expand(a)
            send_expanded(a)

        pass_expanded()

    @pl.when(s > 0)
    def _():
        for d in range(1, replicas):
            src = replica(d)
            remote(q_cols.at[src], q_cols.at[src], q_send.at[0], q_recv.at[src], dp=replica(1)).wait_recv()

    @pl.loop(0, STREAMS)
    def _(a):
        for d in range(1, replicas):
            if d != across:
                e_wait(a, replica(d))

    @pl.when(s == 0)
    def _():
        @pl.loop(0, STREAMS)
        def _(a):
            wait_chunks(tail_in, t2_send, t2_recv, a)
            remote(tail_in.at[a, t], tail_in.at[a, t], t2_send.at[a, 0], t2_recv.at[a, t], tensor=other(1)).wait_recv()
            for k in range(replicas):
                for pair in range(tensors // 2):
                    both = [
                        jnp.concatenate(halves(tail_in[a, o, k].astype(F32)), axis=1)
                        for o in (2 * pair, 2 * pair + 1)
                    ]
                    q_cols[k, a, 16 * pair:16 * pair + 16, :] = jnp.concatenate(both, axis=0).astype(BF16)

    every = replicas * STREAMS * rows
    out_ref[0] = lax.dot_general(
        expanded[...].reshape(every, units), q_cols[...].reshape(every, q_cols.shape[-1]),
        CONTRACT_FIRST, preferred_element_type=F32,
    )

    each_piece(lambda copy: copy.wait_send())
    @pl.when(s > 0)
    def _():
        for d in range(1, replicas):
            q_copy(d).wait_send()

    @pl.loop(0, STREAMS)
    def _(a):
        scatter_sent(f_out, f_in, fs_send, fs_recv, a)
        for copy in (*e_copies(a), *e_passed(a)):
            copy.wait_send()

        @pl.when(s > 0)
        def _():
            send_back(a).wait_send()
            scatter_sent(b_out, b_in, bs_send, bs_recv, a)

        @pl.when(s < last)
        def _():
            for copy in spread(f_sum, hc, fg_send, fg_recv, a, jnp.minimum(s + 1, last)):
                copy.wait_send()

        @pl.when(s == last)
        def _():
            for copy in own_spread(a):
                copy.wait_send()

        @pl.when(s > 1)
        def _():
            for copy in spread(b_sum, qc, bg_send, bg_recv, a, jnp.maximum(s - 1, 0)):
                copy.wait_send()

        @pl.when(s == 1)
        def _():
            for d in range(1, replicas):
                tail_copy(a, d).wait_send()
            for copy in spread(tail_mid, tail_in, t2_send, t2_recv, a, 0):
                copy.wait_send()


def solution(mesh):
    sections, tensors, replicas = (mesh.shape[name] for name in ("section", "tensor", "dp"))

    def shards(x_in, gate_weight, up_weight, down_weight, norm_gain, cotangent):
        features, units = gate_weight.shape[1:]
        rows = 8 * tensors
        width = features // replicas
        half = features // 2
        vmem, dma = pltpu.VMEM, pltpu.SemaphoreType.DMA
        chunks = vmem((STREAMS, tensors, 16, half), BF16)
        chunk = vmem((STREAMS, 16, half), BF16)
        factor = vmem((STREAMS, rows, units), F32)
        pair = [dma((STREAMS, tensors)), dma((STREAMS, tensors))]
        local = pl.BlockSpec(memory_space=pltpu.VMEM)
        anywhere = pl.BlockSpec(memory_space=pl.ANY)
        return pl.pallas_call(
            functools.partial(kernel, (sections, tensors, replicas)),
            out_shape=jax.ShapeDtypeStruct((1, units, width), F32),
            in_specs=[local, local, local, anywhere, anywhere, anywhere],
            out_specs=local,
            scratch_shapes=[
                vmem((features, 2 * units), BF16),
                vmem((units, features), BF16),
                vmem((features, units), BF16),
                vmem((2 * units, features), BF16),
                vmem((sections * tensors, *x_in.shape[:0:-1]), BF16),
                chunks, chunks, chunks,
                vmem((rows, features), BF16),
                vmem((rows, features), F32),
                vmem((STREAMS, rows, units), BF16),
                vmem((rows, 2 * units), BF16),
                factor, factor, factor,
                chunks, chunks, chunks, chunks,
                chunk, chunk,
                vmem((STREAMS, replicas, 16, width // 2), BF16),
                vmem((STREAMS, replicas, 16, width // 2), BF16),
                vmem((STREAMS, tensors, replicas, 16, width // 2), BF16),
                vmem((STREAMS, rows, features), BF16),
                vmem((replicas, STREAMS, rows, width), BF16),
                vmem((replicas, STREAMS, rows, units), BF16),
                dma((3,)),
                dma((2, tensors)), dma((sections * tensors,)),
                *pair, *pair, *pair, *pair,
                dma((STREAMS,)), dma((STREAMS,)),
                *pair,
                dma((STREAMS, replicas)), dma((STREAMS, replicas)),
                dma((replicas,)), dma((replicas,)),
                dma((STREAMS, replicas)), dma((STREAMS, replicas)),
                *pair,
                pltpu.SemaphoreType.REGULAR,
            ],
            compiler_params=pltpu.CompilerParams(
                collective_id=0, has_side_effects=True, vmem_limit_bytes=56 * 1024 * 1024
            ),
            name="expanded_step",
        )(jnp.swapaxes(x_in, 1, 2), jnp.swapaxes(cotangent, 1, 2), norm_gain, gate_weight, up_weight, down_weight)

    placed = (
        P(None, "dp", ("section", "tensor")),
        P("section", None, "tensor"),
        P("section", None, "tensor"),
        P("section", "tensor", None),
        P("section", None),
        P(None, "dp", ("section", "tensor")),
    )
    return jax.shard_map(
        shards, mesh=mesh, in_specs=placed, out_specs=P("section", "tensor", "dp"), check_vma=False
    )
```

```python
import functools

import jax
import jax.numpy as jnp
from jax import lax
from jax.experimental import pallas as pl
from jax.experimental.pallas import tpu as pltpu
from jax.sharding import PartitionSpec as P

EPSILON = 1e-05
F32, BF16 = jnp.float32, jnp.bfloat16
CONTRACT_FIRST = (((0,), (0,)), ((), ()))
STREAMS = 2
PARTS = 2


def dot(left, right):
    return jnp.dot(left, right, preferred_element_type=F32)


def chunked(rows):
    half = rows.shape[1] // 2
    return jnp.concatenate([rows[:, :half], rows[:, half:]], axis=0)


def unchunked(chunk):
    chunk = chunk.astype(F32)
    return jnp.concatenate([chunk[:8], chunk[8:]], axis=1)


def row_sum(values):
    return jnp.sum(values, axis=-1, keepdims=True)


def kernel(
    sizes, x_ref, c_ref, gain_ref, gate_hbm, up_hbm, down_hbm, out_ref,
    gate_up, down, down_t, gate_up_t, landing, hc, hn, qc, normed, product, hidden, slopes,
    gate_factor, up_factor, back_hidden, f_out, f_in, b_out, b_in, f_sum, b_sum, tail_out, tail_mid,
    tail_in, q_rows, q_cols, expanded,
    w_sem, piece_send, piece_recv, fs_send, fs_recv, bs_send, bs_recv, fg_send, fg_recv, bg_send, bg_recv,
    back_send, back_recv, own_send, own_recv, relay_send, relay_recv, rest_send, rest_recv, e_send, e_recv,
    q_send, q_recv, t1_send, t1_recv, t2_send, t2_recv, go,
):
    sections, tensors, replicas = sizes
    s, t, r = lax.axis_index("section"), lax.axis_index("tensor"), lax.axis_index("dp")
    last = sections - 1
    features = down.shape[1]
    span = features // PARTS
    units = down.shape[0]
    rows = normed.shape[0]
    offsets = sorted(range(1, tensors), key=lambda d: (-min(d, tensors - d), d))
    me = s * tensors + t

    def remote(src, dst, send, recv, **where):
        return pltpu.make_async_remote_copy(
            src_ref=src, dst_ref=dst, send_sem=send, recv_sem=recv, device_id=where,
            device_id_type=pl.DeviceIdType.MESH,
        )

    def other(d):
        return lax.rem(t + d, tensors)

    def replica(d):
        return lax.rem(r + d, replicas)

    loads = [
        pltpu.make_async_copy(src.at[0], dst, w_sem.at[i])
        for i, (src, dst) in enumerate(
            ((gate_hbm, gate_up.at[:, :units]), (up_hbm, gate_up.at[:, units:]), (down_hbm, down))
        )
    ]
    for load in loads:
        load.start()

    barrier = pltpu.get_barrier_semaphore()
    for d in range(1, sections * tensors):
        to = lax.rem(me + d, sections * tensors)
        pl.semaphore_signal(
            barrier, inc=1, device_id={"section": to // tensors, "tensor": lax.rem(to, tensors)},
            device_id_type=pl.DeviceIdType.MESH,
        )
    for d in range(1, replicas):
        pl.semaphore_signal(
            barrier, inc=1, device_id={"dp": replica(d)}, device_id_type=pl.DeviceIdType.MESH
        )
    pl.semaphore_wait(barrier, sections * tensors + replicas - 2)

    inputs = (x_ref, c_ref)

    def piece_copy(which, d):
        return remote(
            inputs[which].at[0], landing.at[me], piece_send.at[which, d], piece_recv.at[me],
            section=0 if which == 0 else last, tensor=other(d),
        )

    def each_piece(which, action):
        home = 0 if which == 0 else last
        for d in offsets:
            action(piece_copy(which, d))

        @pl.when(s != home)
        def _():
            action(piece_copy(which, 0))

    each_piece(0, lambda copy: copy.start())

    def gather_pieces(which, dst):
        landing[me] = inputs[which][0]

        @pl.loop(1, sections * tensors)
        def _(d):
            src = lax.rem(me + d, sections * tensors)
            remote(
                inputs[which].at[0], landing.at[src], piece_send.at[which, 0], piece_recv.at[src], tensor=other(1)
            ).wait_recv()

        def block(j):
            return jnp.concatenate([landing[2 * j].astype(F32), landing[2 * j + 1].astype(F32)], axis=0).T

        blocks = span // 256
        for p in range(PARTS):
            for j in range(blocks):
                low, high = block(2 * p * blocks + j), block((2 * p + 1) * blocks + j)
                for a in range(STREAMS):
                    for o in range(tensors):
                        part = slice(a * rows + 8 * o, a * rows + 8 * o + 8)
                        dst[a, p, o, :, 128 * j:128 * j + 128] = jnp.concatenate(
                            [low[part], high[part]], axis=0
                        ).astype(BF16)

    def wait_chunk(buffer, send, recv, a, p, src):
        remote(
            buffer.at[a, p, src], buffer.at[a, p, src], send.at[a, p, 0], recv.at[a, p, src], tensor=other(1)
        ).wait_recv()

    def wait_chunks(buffer, send, recv, a, p):
        for d in (0, *reversed(offsets)):
            wait_chunk(buffer, send, recv, a, p, other(d))

    def columns(p):
        return slice(p * span, (p + 1) * span)

    def gated(buffer, a, ready):
        square, both = 0.0, 0.0
        for p in range(PARTS):
            ready(p)
            gain = gain_ref[:, columns(p)]
            squares = []
            for k in range(tensors // 2):
                pair = [unchunked(buffer[a, p, o]) for o in (2 * k, 2 * k + 1)]
                squares += [row_sum(v * v) for v in pair]
                normed[16 * k:16 * k + 16, columns(p)] = (jnp.concatenate(pair, axis=0) * gain).astype(BF16)
            square = square + jnp.concatenate(squares, axis=0)
            both = both + dot(normed[:, columns(p)], gate_up[columns(p), :])
        both = both * lax.rsqrt(square / features + EPSILON)
        return both[:, :units], both[:, units:]

    def fill_q_rows(a, p):
        for k in range(tensors // 2):
            pair = [unchunked(qc[a, p, o]) for o in (2 * k, 2 * k + 1)]
            q_rows[a, 16 * k:16 * k + 16, columns(p)] = jnp.concatenate(pair, axis=0).astype(BF16)

    def back_product(a, ready):
        total = 0.0
        for p in range(PARTS):
            ready(p)
            fill_q_rows(a, p)
            total = total + dot(q_rows[a, :, columns(p)], down_t[columns(p), :])
        return total

    def fill(out, a, p, left, right):
        product[p] = dot(left, right[:, columns(p)])
        for o in range(tensors):
            out[a, p, o] = chunked(product[p, 8 * o:8 * o + 8, :]).astype(BF16)

    def scatter_copies(out, land, send, recv, a, p):
        return [
            remote(
                out.at[a, p, other(d)], land.at[a, p, t], send.at[a, p, d], recv.at[a, p, t], tensor=other(d)
            )
            for d in offsets
        ]

    def scatter(out, land, send, recv, a, p):
        for copy in scatter_copies(out, land, send, recv, a, p):
            copy.start()

    def summed(out, land, send, recv, a, p):
        total = out[a, p, t].astype(F32)
        for d in reversed(offsets):
            wait_chunk(land, send, recv, a, p, other(d))
            total = total + land[a, p, other(d)].astype(F32)
        return total

    def spread_copies(src, dst, send, recv, a, p, section):
        return [
            remote(
                src.at[a, p], dst.at[a, p, t], send.at[a, p, d], recv.at[a, p, t], section=section,
                tensor=other(d),
            )
            for d in (*offsets, 0)
        ]

    def forward_copies(a, p):
        return spread_copies(f_sum, hc, fg_send, fg_recv, a, p, jnp.minimum(s + 1, last))

    def backward_copies(a, p):
        return spread_copies(b_sum, qc, bg_send, bg_recv, a, p, jnp.maximum(s - 1, 0))

    def own_copies(a, p):
        return spread_copies(b_sum, hn, own_send, own_recv, a, p, last)

    def relay_copy(a):
        return remote(f_out.at[a], b_out.at[a], relay_send.at[a], relay_recv.at[a], section=0, tensor=t)

    def rest_copy(a):
        return remote(hc.at[a, :, t], qc.at[a, :, t], rest_send.at[a], rest_recv.at[a], section=0, tensor=t)

    def send_back(a):
        return remote(
            hc.at[a], hn.at[a], back_send.at[a], back_recv.at[a], section=jnp.maximum(s - 1, 0), tensor=t
        )

    across = replicas // 2
    partner = lax.rem(r + across, replicas)

    def along(d):
        return (r // across) * across + lax.rem(r + d, across)

    def e_copies(a):
        return [
            remote(expanded.at[r, a], expanded.at[r, a], e_send.at[a, d], e_recv.at[a, r], dp=to)
            for d, to in enumerate([partner] + [along(d) for d in range(1, across)])
        ]

    def e_passed(a):
        return [
            remote(
                expanded.at[partner, a], expanded.at[partner, a], e_send.at[a, across + d],
                e_recv.at[a, partner], dp=along(d),
            )
            for d in range(1, across)
        ]

    def e_wait(a, src):
        remote(expanded.at[src, a], expanded.at[src, a], e_send.at[a, 0], e_recv.at[a, src], dp=partner).wait_recv()

    def send_expanded(a):
        for copy in e_copies(a):
            copy.start()

    def pass_expanded():
        @pl.loop(0, STREAMS)
        def _(a):
            e_wait(a, partner)
            for copy in e_passed(a):
                copy.start()

    def q_copy(d):
        width = q_cols.shape[-1]
        columns = pl.ds(pl.multiple_of(replica(d) * width, width), width)
        return remote(q_rows.at[:, :, columns], q_cols.at[r], q_send.at[d], q_recv.at[r], dp=replica(d))

    def send_q():
        width = q_cols.shape[-1]
        for d in range(1, replicas):
            q_copy(d).start()
        q_cols[r] = q_rows[:, :, pl.ds(pl.multiple_of(r * width, width), width)]

    def tail_copy(a, d):
        return remote(
            tail_out.at[a, replica(d)], tail_mid.at[a, r], t1_send.at[a, d], t1_recv.at[a, r], dp=replica(d)
        )

    def tail_spread(a):
        return [
            remote(
                tail_mid.at[a], tail_in.at[a, t], t2_send.at[a, d], t2_recv.at[a, t], section=0, tensor=other(d)
            )
            for d in (*offsets, 0)
        ]

    def owner_backward(a):
        grad = jnp.concatenate(
            [unchunked(summed(b_out, b_in, bs_send, bs_recv, a, p)) for p in range(PARTS)], axis=1
        )
        value = jnp.concatenate([unchunked(hc[a, p, t]) for p in range(PARTS)], axis=1)
        before = jnp.concatenate([unchunked(qc[a, p, t]) for p in range(PARTS)], axis=1)
        scale = lax.rsqrt(row_sum(value * value) / features + EPSILON)
        weighted = grad * gain_ref[...]
        pull = scale * scale * scale * (row_sum(value * weighted) / features)
        return before + scale * weighted - value * pull

    def backward_product(a, incoming):
        slopes[:, :units] = (incoming * gate_factor[a]).astype(BF16)
        slopes[:, units:] = (incoming * up_factor[a]).astype(BF16)
        for p in range(PARTS):
            fill(b_out, a, p, slopes[...], gate_up_t)
            scatter(b_out, b_in, bs_send, bs_recv, a, p)

    def pass_back(a):
        row = owner_backward(a)
        for p in range(PARTS):
            b_sum[a, p] = chunked(row[:, columns(p)]).astype(BF16)
            for copy in backward_copies(a, p):
                copy.start()

    def expand(a, ready):
        gate_new, up_new = gated(hn, a, ready)
        expanded[r, a] = (gate_new / (1.0 + jnp.exp(-gate_new)) * up_new).astype(BF16)

    def allow(section):
        pl.semaphore_signal(
            go, inc=1, device_id={"section": section, "tensor": t}, device_id_type=pl.DeviceIdType.MESH
        )

    for load in loads:
        load.wait()

    @pl.when(s > 0)
    def _():
        @pl.loop(0, features // 256)
        def _(j):
            part = pl.ds(pl.multiple_of(256 * j, 256), 256)
            down_t[part, :] = down[:, part].T
            gate_up_t[:, part] = gate_up[part, :].T

    @pl.when(s > 0)
    def _():
        each_piece(1, lambda copy: copy.start())

    @pl.when(s == last)
    def _():
        gather_pieces(1, qc)

        @pl.loop(0, STREAMS)
        def _(a):
            back_hidden[a] = back_product(a, lambda p: None)

        send_q()

    @pl.when(s == 0)
    def _():
        gather_pieces(0, hc)

    @pl.loop(0, STREAMS)
    def _(a):
        def ready(p):
            @pl.when(s > 0)
            def _():
                wait_chunks(hc, fg_send, fg_recv, a, p)

                if p == PARTS - 1:
                    send_back(a).start()

        gate_pre, up_pre = gated(hc, a, ready)
        sigmoid = 1.0 / (1.0 + jnp.exp(-gate_pre))
        silu = gate_pre * sigmoid
        hidden[a] = (silu * up_pre).astype(BF16)
        up_factor[a] = silu
        gate_factor[a] = up_pre * sigmoid * (1.0 + gate_pre * (1.0 - sigmoid))

        @pl.when(s < last)
        def _():
            for p in range(PARTS):
                fill(f_out, a, p, hidden[a], down)
                scatter(f_out, f_in, fs_send, fs_recv, a, p)

        @pl.when(s == last)
        def _():
            backward_product(a, back_hidden[a])

    @pl.when(s == last)
    def _():
        @pl.loop(0, STREAMS)
        def _(a):
            for p in range(PARTS):
                fill(f_out, a, p, hidden[a], down)
            for copy in (relay_copy(a), rest_copy(a)):
                copy.start()

    @pl.when(s < last)
    def _():
        @pl.loop(0, STREAMS)
        def _(a):
            for p in range(PARTS):
                total = summed(f_out, f_in, fs_send, fs_recv, a, p)
                f_sum[a, p] = (hc[a, p, t].astype(F32) + total).astype(BF16)
                for copy in forward_copies(a, p):
                    copy.start()

        @pl.when(s == 0)
        def _():
            each_piece(1, lambda copy: copy.start())

        @pl.loop(0, STREAMS)
        def _(a):
            send_back(a).wait_recv()

            @pl.when(jnp.logical_and(s == 1, a == STREAMS - 1))
            def _():
                allow(0)

            expand(a, lambda p: None)

            @pl.when(s > 0)
            def _():
                send_expanded(a)

    @pl.when(s == 0)
    def _():
        pl.semaphore_wait(go, 1)

        @pl.loop(0, STREAMS)
        def _(a):
            send_expanded(a)

    @pl.when(s < 2)
    def _():
        pass_expanded()

    @pl.when(s == 0)
    def _():
        @pl.loop(0, STREAMS)
        def _(a):
            relay_copy(a).wait_recv()
            for p in range(PARTS):
                scatter(b_out, b_in, bs_send, bs_recv, a, p)

        @pl.loop(0, STREAMS)
        def _(a):
            rest_copy(a).wait_recv()
            for p in range(PARTS):
                total = summed(b_out, b_in, bs_send, bs_recv, a, p)
                b_sum[a, p] = (qc[a, p, t].astype(F32) + total).astype(BF16)
                for copy in own_copies(a, p):
                    copy.start()

    @pl.when(jnp.logical_and(s > 0, s < last))
    def _():
        @pl.loop(0, STREAMS)
        def _(a):
            backward_product(
                a, back_product(a, lambda p: wait_chunks(qc, bg_send, bg_recv, a, p))
            )

        send_q()

    @pl.when(s > 1)
    def _():
        @pl.loop(0, STREAMS)
        def _(a):
            pass_back(a)

    @pl.when(s == 2)
    def _():
        pass_expanded()

    @pl.when(s == 1)
    def _():
        @pl.loop(0, STREAMS)
        def _(a):
            row = owner_backward(a)
            width = q_cols.shape[-1]
            for k in range(replicas):
                tail_out[a, k] = chunked(row[:, k * width:(k + 1) * width]).astype(BF16)
            for d in range(1, replicas):
                tail_copy(a, d).start()
            tail_mid[a, r] = tail_out[a, r]

        @pl.loop(0, STREAMS)
        def _(a):
            for d in range(1, replicas):
                src = replica(d)
                remote(
                    tail_mid.at[a, src], tail_mid.at[a, src], t1_send.at[a, 0], t1_recv.at[a, src], dp=replica(1)
                ).wait_recv()
            for copy in tail_spread(a):
                copy.start()

    @pl.when(s == last)
    def _():
        @pl.loop(0, STREAMS)
        def _(a):
            expand(a, lambda p: wait_chunks(hn, own_send, own_recv, a, p))
            send_expanded(a)

        pass_expanded()

    @pl.when(s > 0)
    def _():
        for d in range(1, replicas):
            src = replica(d)
            remote(q_cols.at[src], q_cols.at[src], q_send.at[0], q_recv.at[src], dp=replica(1)).wait_recv()

    @pl.loop(0, STREAMS)
    def _(a):
        for d in range(1, replicas):
            if d != across:
                e_wait(a, replica(d))

    @pl.when(s == 0)
    def _():
        @pl.loop(0, STREAMS)
        def _(a):
            for d in (0, *reversed(offsets)):
                src = other(d)
                remote(
                    tail_in.at[a, src], tail_in.at[a, src], t2_send.at[a, 0], t2_recv.at[a, src], tensor=other(1)
                ).wait_recv()
            for k in range(replicas):
                for pair in range(tensors // 2):
                    both = [
                        unchunked(tail_in[a, o, k]) for o in (2 * pair, 2 * pair + 1)
                    ]
                    q_cols[k, a, 16 * pair:16 * pair + 16, :] = jnp.concatenate(both, axis=0).astype(BF16)

    every = replicas * STREAMS * rows
    out_ref[0] = lax.dot_general(
        expanded[...].reshape(every, units), q_cols[...].reshape(every, q_cols.shape[-1]),
        CONTRACT_FIRST, preferred_element_type=F32,
    )

    for which in (0, 1):
        each_piece(which, lambda copy: copy.wait_send())

    @pl.when(s > 0)
    def _():
        for d in range(1, replicas):
            q_copy(d).wait_send()

    @pl.loop(0, STREAMS)
    def _(a):
        for copy in (*e_copies(a), *e_passed(a)):
            copy.wait_send()

        for p in range(PARTS):
            for copy in scatter_copies(b_out, b_in, bs_send, bs_recv, a, p):
                copy.wait_send()

            @pl.when(s < last)
            def _():
                for copy in (*scatter_copies(f_out, f_in, fs_send, fs_recv, a, p), *forward_copies(a, p)):
                    copy.wait_send()

            @pl.when(s > 1)
            def _():
                for copy in backward_copies(a, p):
                    copy.wait_send()

            @pl.when(s == 0)
            def _():
                for copy in own_copies(a, p):
                    copy.wait_send()

        @pl.when(s > 0)
        def _():
            send_back(a).wait_send()

        @pl.when(s == last)
        def _():
            for copy in (relay_copy(a), rest_copy(a)):
                copy.wait_send()

        @pl.when(s == 1)
        def _():
            for d in range(1, replicas):
                tail_copy(a, d).wait_send()
            for copy in tail_spread(a):
                copy.wait_send()


def solution(mesh):
    sections, tensors, replicas = (mesh.shape[name] for name in ("section", "tensor", "dp"))

    def shards(x_in, gate_weight, up_weight, down_weight, norm_gain, cotangent):
        features, units = gate_weight.shape[1:]
        rows = 8 * tensors
        width = features // replicas
        span = features // PARTS
        vmem, dma = pltpu.VMEM, pltpu.SemaphoreType.DMA
        chunks = vmem((STREAMS, PARTS, tensors, 16, span // 2), BF16)
        chunk = vmem((STREAMS, PARTS, 16, span // 2), BF16)
        factor = vmem((STREAMS, rows, units), F32)
        pair = [dma((STREAMS, PARTS, tensors))] * 2
        stream = [dma((STREAMS,))] * 2
        flat = [dma((STREAMS, tensors))] * 2
        local = pl.BlockSpec(memory_space=pltpu.VMEM)
        anywhere = pl.BlockSpec(memory_space=pl.ANY)
        return pl.pallas_call(
            functools.partial(kernel, (sections, tensors, replicas)),
            out_shape=jax.ShapeDtypeStruct((1, units, width), F32),
            in_specs=[local, local, local, anywhere, anywhere, anywhere],
            out_specs=local,
            scratch_shapes=[
                vmem((features, 2 * units), BF16),
                vmem((units, features), BF16),
                vmem((features, units), BF16),
                vmem((2 * units, features), BF16),
                vmem((sections * tensors, *x_in.shape[:0:-1]), BF16),
                chunks, chunks, chunks,
                vmem((rows, features), BF16),
                vmem((PARTS, rows, span), F32),
                vmem((STREAMS, rows, units), BF16),
                vmem((rows, 2 * units), BF16),
                factor, factor, factor,
                chunks, chunks, chunks, chunks,
                chunk, chunk,
                vmem((STREAMS, replicas, 16, width // 2), BF16),
                vmem((STREAMS, replicas, 16, width // 2), BF16),
                vmem((STREAMS, tensors, replicas, 16, width // 2), BF16),
                vmem((STREAMS, rows, features), BF16),
                vmem((replicas, STREAMS, rows, width), BF16),
                vmem((replicas, STREAMS, rows, units), BF16),
                dma((3,)),
                dma((2, tensors)), dma((sections * tensors,)),
                *pair, *pair, *pair, *pair,
                *stream,
                *pair,
                *stream, *stream,
                dma((STREAMS, replicas)), dma((STREAMS, replicas)),
                dma((replicas,)), dma((replicas,)),
                dma((STREAMS, replicas)), dma((STREAMS, replicas)),
                *flat,
                pltpu.SemaphoreType.REGULAR,
            ],
            compiler_params=pltpu.CompilerParams(
                collective_id=0, has_side_effects=True, vmem_limit_bytes=56 * 1024 * 1024
            ),
            name="expanded_step",
        )(jnp.swapaxes(x_in, 1, 2), jnp.swapaxes(cotangent, 1, 2), norm_gain, gate_weight, up_weight, down_weight)

    placed = (
        P(None, "dp", ("section", "tensor")),
        P("section", None, "tensor"),
        P("section", None, "tensor"),
        P("section", "tensor", None),
        P("section", None),
        P(None, "dp", ("section", "tensor")),
    )
    return jax.shard_map(
        shards, mesh=mesh, in_specs=placed, out_specs=P("section", "tensor", "dp"), check_vma=False
    )
```

```python
import functools

import jax
import jax.numpy as jnp
from jax import lax
from jax.experimental import pallas as pl
from jax.experimental.pallas import tpu as pltpu
from jax.sharding import PartitionSpec as P

EPSILON = 1e-05
F32, BF16 = jnp.float32, jnp.bfloat16
CONTRACT_FIRST = (((0,), (0,)), ((), ()))
STREAMS = 2
PARTS = 2


def dot(left, right):
    return jnp.dot(left, right, preferred_element_type=F32)


def chunked(rows):
    half = rows.shape[1] // 2
    return jnp.concatenate([rows[:, :half], rows[:, half:]], axis=0)


def unchunked(chunk):
    chunk = chunk.astype(F32)
    return jnp.concatenate([chunk[:8], chunk[8:]], axis=1)


def row_sum(values):
    return jnp.sum(values, axis=-1, keepdims=True)


def kernel(
    sizes, x_ref, c_ref, gain_hbm, gate_hbm, up_hbm, down_hbm, out_ref,
    gain_ref, gate_up, down, down_t, gate_up_t, landing, hc, hn, qc, normed, product, hidden, slopes,
    gate_factor, up_factor, back_hidden, f_out, f_in, b_out, b_in, f_sum, b_sum, tail_out, tail_mid,
    tail_in, q_rows, q_cols, expanded,
    w_sem, piece_send, piece_recv, fs_send, fs_recv, bs_send, bs_recv, fg_send, fg_recv, bg_send, bg_recv,
    back_send, back_recv, own_send, own_recv, relay_send, relay_recv, rest_send, rest_recv, e_send, e_recv,
    q_send, q_recv, t1_send, t1_recv, t2_send, t2_recv, go,
):
    sections, tensors, replicas = sizes
    s, t, r = lax.axis_index("section"), lax.axis_index("tensor"), lax.axis_index("dp")
    last = sections - 1
    features = down.shape[1]
    span = features // PARTS
    units = down.shape[0]
    rows = normed.shape[0]
    offsets = sorted(range(1, tensors), key=lambda d: (-min(d, tensors - d), d))
    me = s * tensors + t

    def remote(src, dst, send, recv, **where):
        return pltpu.make_async_remote_copy(
            src_ref=src, dst_ref=dst, send_sem=send, recv_sem=recv, device_id=where,
            device_id_type=pl.DeviceIdType.MESH,
        )

    def other(d):
        return lax.rem(t + d, tensors)

    def replica(d):
        return lax.rem(r + d, replicas)

    loads = [
        pltpu.make_async_copy(src, dst, w_sem.at[i])
        for i, (src, dst) in enumerate((
            (gain_hbm, gain_ref), (gate_hbm.at[0], gate_up.at[:, :units]), (up_hbm.at[0], gate_up.at[:, units:]),
            (down_hbm.at[0], down),
        ))
    ]
    for load in loads:
        load.start()

    barrier = pltpu.get_barrier_semaphore()
    for d in (*offsets, 0):
        for k in range(sections):
            if d or k:
                pl.semaphore_signal(
                    barrier, inc=1, device_id={"section": lax.rem(s + k, sections), "tensor": other(d)},
                    device_id_type=pl.DeviceIdType.MESH,
                )
        if d == offsets[0]:
            for k in range(1, replicas):
                pl.semaphore_signal(
                    barrier, inc=1, device_id={"dp": replica(k)}, device_id_type=pl.DeviceIdType.MESH
                )
    pl.semaphore_wait(barrier, sections * tensors + replicas - 2)

    inputs = (x_ref, c_ref)

    def piece_copy(which, d):
        return remote(
            inputs[which].at[0], landing.at[me], piece_send.at[which, d], piece_recv.at[me],
            section=0 if which == 0 else last, tensor=other(d),
        )

    def each_piece(which, action):
        home = 0 if which == 0 else last
        for d in offsets:
            action(piece_copy(which, d))

        @pl.when(s != home)
        def _():
            action(piece_copy(which, 0))

    each_piece(0, lambda copy: copy.start())

    def own_piece(which):
        return pltpu.make_async_copy(inputs[which].at[0], landing.at[me], piece_recv.at[me])

    @pl.when(s == 0)
    def _():
        own_piece(0).start()

    @pl.when(s == last)
    def _():
        own_piece(1).start()

    def gather_pieces(which, dst, p):
        count = sections * tensors // PARTS

        @pl.loop(p * count, (p + 1) * count)
        def _(src):
            @pl.when(src == me)
            def _():
                own_piece(which).wait()

            @pl.when(src != me)
            def _():
                remote(
                    inputs[which].at[0], landing.at[src], piece_send.at[which, 0], piece_recv.at[src],
                    tensor=other(1),
                ).wait_recv()

        def block(j):
            return jnp.concatenate([landing[2 * j].astype(F32), landing[2 * j + 1].astype(F32)], axis=0).T

        blocks = span // 256
        for j in range(blocks):
            low, high = block(2 * p * blocks + j), block((2 * p + 1) * blocks + j)
            for a in range(STREAMS):
                for o in range(tensors):
                    part = slice(a * rows + 8 * o, a * rows + 8 * o + 8)
                    dst[a, p, o, :, 128 * j:128 * j + 128] = jnp.concatenate(
                        [low[part], high[part]], axis=0
                    ).astype(BF16)

    def wait_chunk(buffer, send, recv, a, p, src):
        remote(
            buffer.at[a, p, src], buffer.at[a, p, src], send.at[a, p, 0], recv.at[a, p, src], tensor=other(1)
        ).wait_recv()

    def wait_chunks(buffer, send, recv, a, p):
        for d in (0, *reversed(offsets)):
            wait_chunk(buffer, send, recv, a, p, other(d))

    def columns(p):
        return slice(p * span, (p + 1) * span)

    def gated(buffer, a, ready):
        square, both = 0.0, 0.0
        for p in range(PARTS):
            ready(p)
            gain = gain_ref[:, columns(p)]
            squares = []
            for k in range(tensors // 2):
                pair = [unchunked(buffer[a, p, o]) for o in (2 * k, 2 * k + 1)]
                squares += [row_sum(v * v) for v in pair]
                normed[16 * k:16 * k + 16, columns(p)] = (jnp.concatenate(pair, axis=0) * gain).astype(BF16)
            square = square + jnp.concatenate(squares, axis=0)
            both = both + dot(normed[:, columns(p)], gate_up[columns(p), :])
        both = both * lax.rsqrt(square / features + EPSILON)
        return both[:, :units], both[:, units:]

    def fill_q_rows(a, p):
        for k in range(tensors // 2):
            pair = [unchunked(qc[a, p, o]) for o in (2 * k, 2 * k + 1)]
            q_rows[a, 16 * k:16 * k + 16, columns(p)] = jnp.concatenate(pair, axis=0).astype(BF16)

    def back_product(a, ready):
        total = 0.0
        for p in range(PARTS):
            ready(p)
            fill_q_rows(a, p)
            total = total + dot(q_rows[a, :, columns(p)], down_t[columns(p), :])
        return total

    def fill(out, a, p, left, right):
        product[p] = dot(left, right[:, columns(p)])
        for o in range(tensors):
            out[a, p, o] = chunked(product[p, 8 * o:8 * o + 8, :]).astype(BF16)

    def scatter_copies(out, land, send, recv, a, p):
        return [
            remote(
                out.at[a, p, other(d)], land.at[a, p, t], send.at[a, p, d], recv.at[a, p, t], tensor=other(d)
            )
            for d in offsets
        ]

    def scatter(out, land, send, recv, a, p):
        for copy in scatter_copies(out, land, send, recv, a, p):
            copy.start()

    def summed(out, land, send, recv, a, p):
        total = out[a, p, t].astype(F32)
        for d in reversed(offsets):
            wait_chunk(land, send, recv, a, p, other(d))
            total = total + land[a, p, other(d)].astype(F32)
        return total

    def spread_copies(src, dst, send, recv, a, p, section):
        return [
            remote(
                src.at[a, p], dst.at[a, p, t], send.at[a, p, d], recv.at[a, p, t], section=section,
                tensor=other(d),
            )
            for d in (*offsets, 0)
        ]

    def forward_copies(a, p):
        return spread_copies(f_sum, hc, fg_send, fg_recv, a, p, jnp.minimum(s + 1, last))

    def backward_copies(a, p):
        return spread_copies(b_sum, qc, bg_send, bg_recv, a, p, jnp.maximum(s - 1, 0))

    def own_copies(a, p):
        return spread_copies(b_sum, hn, own_send, own_recv, a, p, last)

    def relay_copy(a):
        return remote(f_out.at[a], b_out.at[a], relay_send.at[a], relay_recv.at[a], section=0, tensor=t)

    def rest_copy(a):
        return remote(hc.at[a, :, t], qc.at[a, :, t], rest_send.at[a], rest_recv.at[a], section=0, tensor=t)

    def send_back(a):
        return remote(
            hc.at[a], hn.at[a], back_send.at[a], back_recv.at[a], section=jnp.maximum(s - 1, 0), tensor=t
        )

    across = replicas // 2
    partner = lax.rem(r + across, replicas)

    def along(d):
        return (r // across) * across + lax.rem(r + d, across)

    def e_copies(a):
        return [
            remote(expanded.at[r, a], expanded.at[r, a], e_send.at[a, d], e_recv.at[a, r], dp=to)
            for d, to in enumerate([partner] + [along(d) for d in range(1, across)])
        ]

    def e_passed(a):
        return [
            remote(
                expanded.at[partner, a], expanded.at[partner, a], e_send.at[a, across + d],
                e_recv.at[a, partner], dp=along(d),
            )
            for d in range(1, across)
        ]

    def e_wait(a, src):
        remote(expanded.at[src, a], expanded.at[src, a], e_send.at[a, 0], e_recv.at[a, src], dp=partner).wait_recv()

    def send_expanded(a):
        for copy in e_copies(a):
            copy.start()

    def pass_expanded():
        @pl.loop(0, STREAMS)
        def _(a):
            e_wait(a, partner)
            for copy in e_passed(a):
                copy.start()

    def q_copy(d):
        width = q_cols.shape[-1]
        columns = pl.ds(pl.multiple_of(replica(d) * width, width), width)
        return remote(q_rows.at[:, :, columns], q_cols.at[r], q_send.at[d], q_recv.at[r], dp=replica(d))

    def send_q():
        width = q_cols.shape[-1]
        for d in range(1, replicas):
            q_copy(d).start()
        q_cols[r] = q_rows[:, :, pl.ds(pl.multiple_of(r * width, width), width)]

    def tail_copy(a, d):
        return remote(
            tail_out.at[a, replica(d)], tail_mid.at[a, r], t1_send.at[a, d], t1_recv.at[a, r], dp=replica(d)
        )

    def tail_spread(a):
        return [
            remote(
                tail_mid.at[a], tail_in.at[a, t], t2_send.at[a, d], t2_recv.at[a, t], section=0, tensor=other(d)
            )
            for d in (*offsets, 0)
        ]

    def owner_backward(a):
        grad = jnp.concatenate(
            [unchunked(summed(b_out, b_in, bs_send, bs_recv, a, p)) for p in range(PARTS)], axis=1
        )
        value = jnp.concatenate([unchunked(hc[a, p, t]) for p in range(PARTS)], axis=1)
        before = jnp.concatenate([unchunked(qc[a, p, t]) for p in range(PARTS)], axis=1)
        scale = lax.rsqrt(row_sum(value * value) / features + EPSILON)
        weighted = grad * gain_ref[...]
        pull = scale * scale * scale * (row_sum(value * weighted) / features)
        return before + scale * weighted - value * pull

    def backward_product(a, incoming):
        slopes[:, :units] = (incoming * gate_factor[a]).astype(BF16)
        slopes[:, units:] = (incoming * up_factor[a]).astype(BF16)
        for p in range(PARTS):
            fill(b_out, a, p, slopes[...], gate_up_t)
            scatter(b_out, b_in, bs_send, bs_recv, a, p)

    def pass_back(a):
        row = owner_backward(a)
        for p in range(PARTS):
            b_sum[a, p] = chunked(row[:, columns(p)]).astype(BF16)
            for copy in backward_copies(a, p):
                copy.start()

    def expand(a, ready):
        gate_new, up_new = gated(hn, a, ready)
        expanded[r, a] = (gate_new / (1.0 + jnp.exp(-gate_new)) * up_new).astype(BF16)

    def forward_sent():
        for which in (0, 1):
            each_piece(which, lambda copy: copy.wait_send())

        @pl.loop(0, STREAMS)
        def _(a):
            for copy in e_copies(a):
                copy.wait_send()

            @pl.when(s > 0)
            def _():
                send_back(a).wait_send()

            @pl.when(s < last)
            def _():
                for p in range(PARTS):
                    for copy in (*scatter_copies(f_out, f_in, fs_send, fs_recv, a, p), *forward_copies(a, p)):
                        copy.wait_send()

    def passed_sent():
        @pl.loop(0, STREAMS)
        def _(a):
            for copy in e_passed(a):
                copy.wait_send()

    def allow(section):
        pl.semaphore_signal(
            go, inc=1, device_id={"section": section, "tensor": t}, device_id_type=pl.DeviceIdType.MESH
        )

    for load in loads:
        load.wait()

    @pl.when(s > 0)
    def _():
        @pl.loop(0, features // 256)
        def _(j):
            part = pl.ds(pl.multiple_of(256 * j, 256), 256)
            down_t[part, :] = down[:, part].T
            gate_up_t[:, part] = gate_up[part, :].T

    @pl.when(s > 0)
    def _():
        each_piece(1, lambda copy: copy.start())

    @pl.when(s == last)
    def _():
        for p in range(PARTS):
            gather_pieces(1, qc, p)

        @pl.loop(0, STREAMS)
        def _(a):
            back_hidden[a] = back_product(a, lambda p: None)

        send_q()

    @pl.loop(0, STREAMS)
    def _(a):
        def ready(p):
            @pl.when(jnp.logical_and(s == 0, a == 0))
            def _():
                gather_pieces(0, hc, p)

            @pl.when(s > 0)
            def _():
                wait_chunks(hc, fg_send, fg_recv, a, p)

                if p == PARTS - 1:
                    send_back(a).start()

        gate_pre, up_pre = gated(hc, a, ready)
        sigmoid = 1.0 / (1.0 + jnp.exp(-gate_pre))
        silu = gate_pre * sigmoid
        hidden[a] = (silu * up_pre).astype(BF16)
        up_factor[a] = silu
        gate_factor[a] = up_pre * sigmoid * (1.0 + gate_pre * (1.0 - sigmoid))

        @pl.when(s < last)
        def _():
            for p in range(PARTS):
                fill(f_out, a, p, hidden[a], down)
                scatter(f_out, f_in, fs_send, fs_recv, a, p)

        @pl.when(s == last)
        def _():
            backward_product(a, back_hidden[a])

    @pl.when(s == last)
    def _():
        @pl.loop(0, STREAMS)
        def _(a):
            for p in range(PARTS):
                fill(f_out, a, p, hidden[a], down)
            for copy in (relay_copy(a), rest_copy(a)):
                copy.start()

    @pl.when(s < last)
    def _():
        @pl.loop(0, STREAMS)
        def _(a):
            for p in range(PARTS):
                total = summed(f_out, f_in, fs_send, fs_recv, a, p)
                f_sum[a, p] = (hc[a, p, t].astype(F32) + total).astype(BF16)
                for copy in forward_copies(a, p):
                    copy.start()

        @pl.when(s == 0)
        def _():
            each_piece(1, lambda copy: copy.start())

        @pl.loop(0, STREAMS)
        def _(a):
            send_back(a).wait_recv()

            @pl.when(jnp.logical_and(s == 1, a == STREAMS - 1))
            def _():
                allow(0)

            expand(a, lambda p: None)

            @pl.when(s > 0)
            def _():
                send_expanded(a)

    @pl.when(s == 0)
    def _():
        pl.semaphore_wait(go, 1)

        @pl.loop(0, STREAMS)
        def _(a):
            send_expanded(a)

    @pl.when(s < 2)
    def _():
        pass_expanded()
        passed_sent()

    @pl.when(s < last)
    def _():
        forward_sent()

    @pl.when(s == 0)
    def _():
        @pl.loop(0, STREAMS)
        def _(a):
            relay_copy(a).wait_recv()
            for p in range(PARTS):
                scatter(b_out, b_in, bs_send, bs_recv, a, p)

        @pl.loop(0, STREAMS)
        def _(a):
            rest_copy(a).wait_recv()
            for p in range(PARTS):
                total = summed(b_out, b_in, bs_send, bs_recv, a, p)
                b_sum[a, p] = (qc[a, p, t].astype(F32) + total).astype(BF16)
                for copy in own_copies(a, p):
                    copy.start()

        @pl.loop(0, STREAMS)
        def _(a):
            for p in range(PARTS):
                for copy in (*scatter_copies(b_out, b_in, bs_send, bs_recv, a, p), *own_copies(a, p)):
                    copy.wait_send()

    @pl.when(jnp.logical_and(s > 0, s < last))
    def _():
        @pl.loop(0, STREAMS)
        def _(a):
            backward_product(
                a, back_product(a, lambda p: wait_chunks(qc, bg_send, bg_recv, a, p))
            )

        send_q()

    @pl.when(s > 1)
    def _():
        @pl.loop(0, STREAMS)
        def _(a):
            pass_back(a)

    @pl.when(s == 2)
    def _():
        pass_expanded()

    @pl.when(s == 1)
    def _():
        @pl.loop(0, STREAMS)
        def _(a):
            row = owner_backward(a)
            width = q_cols.shape[-1]
            for k in range(replicas):
                tail_out[a, k] = chunked(row[:, k * width:(k + 1) * width]).astype(BF16)
            for d in range(1, replicas):
                tail_copy(a, d).start()
            tail_mid[a, r] = tail_out[a, r]

        @pl.loop(0, STREAMS)
        def _(a):
            for d in range(1, replicas):
                src = replica(d)
                remote(
                    tail_mid.at[a, src], tail_mid.at[a, src], t1_send.at[a, 0], t1_recv.at[a, src], dp=replica(1)
                ).wait_recv()
            for copy in tail_spread(a):
                copy.start()

    @pl.when(s == last)
    def _():
        @pl.loop(0, STREAMS)
        def _(a):
            expand(a, lambda p: wait_chunks(hn, own_send, own_recv, a, p))
            send_expanded(a)

        pass_expanded()

    @pl.when(s > 0)
    def _():
        for d in range(1, replicas):
            src = replica(d)
            remote(q_cols.at[src], q_cols.at[src], q_send.at[0], q_recv.at[src], dp=replica(1)).wait_recv()

    @pl.loop(0, STREAMS)
    def _(a):
        for d in range(1, replicas):
            if d != across:
                e_wait(a, replica(d))

    @pl.when(s == 0)
    def _():
        @pl.loop(0, STREAMS)
        def _(a):
            for d in (0, *reversed(offsets)):
                src = other(d)
                remote(
                    tail_in.at[a, src], tail_in.at[a, src], t2_send.at[a, 0], t2_recv.at[a, src], tensor=other(1)
                ).wait_recv()
            for k in range(replicas):
                for pair in range(tensors // 2):
                    both = [
                        unchunked(tail_in[a, o, k]) for o in (2 * pair, 2 * pair + 1)
                    ]
                    q_cols[k, a, 16 * pair:16 * pair + 16, :] = jnp.concatenate(both, axis=0).astype(BF16)

    every = replicas * STREAMS * rows
    out_ref[0] = lax.dot_general(
        expanded[...].reshape(every, units), q_cols[...].reshape(every, q_cols.shape[-1]),
        CONTRACT_FIRST, preferred_element_type=F32,
    )

    @pl.when(s == last)
    def _():
        forward_sent()

    @pl.when(s > 1)
    def _():
        passed_sent()

    @pl.when(s > 0)
    def _():
        for d in range(1, replicas):
            q_copy(d).wait_send()

        @pl.loop(0, STREAMS)
        def _(a):
            for p in range(PARTS):
                for copy in scatter_copies(b_out, b_in, bs_send, bs_recv, a, p):
                    copy.wait_send()

                @pl.when(s > 1)
                def _():
                    for copy in backward_copies(a, p):
                        copy.wait_send()

            @pl.when(s == last)
            def _():
                for copy in (relay_copy(a), rest_copy(a)):
                    copy.wait_send()

            @pl.when(s == 1)
            def _():
                for d in range(1, replicas):
                    tail_copy(a, d).wait_send()
                for copy in tail_spread(a):
                    copy.wait_send()


def solution(mesh):
    sections, tensors, replicas = (mesh.shape[name] for name in ("section", "tensor", "dp"))

    def shards(x_in, gate_weight, up_weight, down_weight, norm_gain, cotangent):
        features, units = gate_weight.shape[1:]
        rows = 8 * tensors
        width = features // replicas
        span = features // PARTS
        vmem, dma = pltpu.VMEM, pltpu.SemaphoreType.DMA
        chunks = vmem((STREAMS, PARTS, tensors, 16, span // 2), BF16)
        chunk = vmem((STREAMS, PARTS, 16, span // 2), BF16)
        factor = vmem((STREAMS, rows, units), F32)
        pair = [dma((STREAMS, PARTS, tensors))] * 2
        stream = [dma((STREAMS,))] * 2
        flat = [dma((STREAMS, tensors))] * 2
        local = pl.BlockSpec(memory_space=pltpu.VMEM)
        anywhere = pl.BlockSpec(memory_space=pl.ANY)
        return pl.pallas_call(
            functools.partial(kernel, (sections, tensors, replicas)),
            out_shape=vmem((1, units, width), F32),
            in_specs=[anywhere] * 6,
            out_specs=local,
            scratch_shapes=[
                vmem((1, features), F32),
                vmem((features, 2 * units), BF16),
                vmem((units, features), BF16),
                vmem((features, units), BF16),
                vmem((2 * units, features), BF16),
                vmem((sections * tensors, *x_in.shape[:0:-1]), BF16),
                chunks, chunks, chunks,
                vmem((rows, features), BF16),
                vmem((PARTS, rows, span), F32),
                vmem((STREAMS, rows, units), BF16),
                vmem((rows, 2 * units), BF16),
                factor, factor, factor,
                chunks, chunks, chunks, chunks,
                chunk, chunk,
                vmem((STREAMS, replicas, 16, width // 2), BF16),
                vmem((STREAMS, replicas, 16, width // 2), BF16),
                vmem((STREAMS, tensors, replicas, 16, width // 2), BF16),
                vmem((STREAMS, rows, features), BF16),
                vmem((replicas, STREAMS, rows, width), BF16),
                vmem((replicas, STREAMS, rows, units), BF16),
                dma((4,)),
                dma((2, tensors)), dma((sections * tensors,)),
                *pair, *pair, *pair, *pair,
                *stream,
                *pair,
                *stream, *stream,
                dma((STREAMS, replicas)), dma((STREAMS, replicas)),
                dma((replicas,)), dma((replicas,)),
                dma((STREAMS, replicas)), dma((STREAMS, replicas)),
                *flat,
                pltpu.SemaphoreType.REGULAR,
            ],
            compiler_params=pltpu.CompilerParams(
                collective_id=0, has_side_effects=True, vmem_limit_bytes=56 * 1024 * 1024
            ),
            name="expanded_step",
        )(jnp.swapaxes(x_in, 1, 2), jnp.swapaxes(cotangent, 1, 2), norm_gain, gate_weight, up_weight, down_weight)

    placed = (
        P(None, "dp", ("section", "tensor")),
        P("section", None, "tensor"),
        P("section", None, "tensor"),
        P("section", "tensor", None),
        P("section", None),
        P(None, "dp", ("section", "tensor")),
    )
    return jax.shard_map(
        shards, mesh=mesh, in_specs=placed, out_specs=P("section", "tensor", "dp"), check_vma=False
    )
```

```python
import functools

import jax
import jax.numpy as jnp
from jax import lax
from jax.experimental import pallas as pl
from jax.experimental.pallas import tpu as pltpu
from jax.sharding import PartitionSpec as P

EPSILON = 1e-05
F32, BF16 = jnp.float32, jnp.bfloat16
CONTRACT_FIRST = (((0,), (0,)), ((), ()))
STREAMS = 2
PARTS = 2


def dot(left, right):
    return jnp.dot(left, right, preferred_element_type=F32)


def chunked(rows):
    half = rows.shape[1] // 2
    return jnp.concatenate([rows[:, :half], rows[:, half:]], axis=0)


def unchunked(chunk):
    chunk = chunk.astype(F32)
    return jnp.concatenate([chunk[:8], chunk[8:]], axis=1)


def row_sum(values):
    return jnp.sum(values, axis=-1, keepdims=True)


def kernel(
    sizes, x_ref, c_ref, gain_hbm, gate_hbm, up_hbm, down_hbm, out_ref,
    gain_ref, both, back, square, gate_up, down, down_t, gate_up_t, landing, hc, hn, qc, normed, product, hidden, slopes,
    gate_factor, up_factor, back_hidden, f_out, f_in, b_out, b_in, f_sum, b_sum, tail_out, tail_mid,
    tail_in, q_rows, q_cols, expanded,
    w_sem, piece_send, piece_recv, fs_send, fs_recv, bs_send, bs_recv, fg_send, fg_recv, bg_send, bg_recv,
    back_send, back_recv, own_send, own_recv, relay_send, relay_recv, rest_send, rest_recv, e_send, e_recv,
    q_send, q_recv, t1_send, t1_recv, t2_send, t2_recv, go,
):
    sections, tensors, replicas = sizes
    s, t, r = lax.axis_index("section"), lax.axis_index("tensor"), lax.axis_index("dp")
    last = sections - 1
    features = down.shape[1]
    span = features // PARTS
    units = down.shape[0]
    rows = normed.shape[0]
    offsets = sorted(range(1, tensors), key=lambda d: (-min(d, tensors - d), d))
    me = s * tensors + t

    def remote(src, dst, send, recv, **where):
        return pltpu.make_async_remote_copy(
            src_ref=src, dst_ref=dst, send_sem=send, recv_sem=recv, device_id=where,
            device_id_type=pl.DeviceIdType.MESH,
        )

    def other(d):
        return lax.rem(t + d, tensors)

    def replica(d):
        return lax.rem(r + d, replicas)

    loads = [
        pltpu.make_async_copy(src, dst, w_sem.at[i])
        for i, (src, dst) in enumerate((
            (gain_hbm, gain_ref), (gate_hbm.at[0], gate_up.at[:, :units]), (up_hbm.at[0], gate_up.at[:, units:]),
            (down_hbm.at[0], down),
        ))
    ]
    for load in loads:
        load.start()

    barrier = pltpu.get_barrier_semaphore()
    for d in (*offsets, 0):
        for k in range(sections):
            if d or k:
                pl.semaphore_signal(
                    barrier, inc=1, device_id={"section": lax.rem(s + k, sections), "tensor": other(d)},
                    device_id_type=pl.DeviceIdType.MESH,
                )
        if d == offsets[0]:
            for k in range(1, replicas):
                pl.semaphore_signal(
                    barrier, inc=1, device_id={"dp": replica(k)}, device_id_type=pl.DeviceIdType.MESH
                )
    pl.semaphore_wait(barrier, sections * tensors + replicas - 2)

    inputs = (x_ref, c_ref)

    def piece_copy(which, d):
        return remote(
            inputs[which].at[0], landing.at[me], piece_send.at[which, d], piece_recv.at[me],
            section=0 if which == 0 else last, tensor=other(d),
        )

    def each_piece(which, action):
        home = 0 if which == 0 else last
        for d in offsets:
            action(piece_copy(which, d))

        @pl.when(s != home)
        def _():
            action(piece_copy(which, 0))

    each_piece(0, lambda copy: copy.start())

    def own_piece(which):
        return pltpu.make_async_copy(inputs[which].at[0], landing.at[me], piece_recv.at[me])

    @pl.when(s == 0)
    def _():
        own_piece(0).start()

    @pl.when(s == last)
    def _():
        own_piece(1).start()

    def gather_pieces(which, dst, p):
        count = sections * tensors // PARTS

        @pl.loop(p * count, (p + 1) * count)
        def _(src):
            @pl.when(src == me)
            def _():
                own_piece(which).wait()

            @pl.when(src != me)
            def _():
                remote(
                    inputs[which].at[0], landing.at[src], piece_send.at[which, 0], piece_recv.at[src],
                    tensor=other(1),
                ).wait_recv()

        def block(j):
            return jnp.concatenate([landing[2 * j].astype(F32), landing[2 * j + 1].astype(F32)], axis=0).T

        blocks = span // 256
        for j in range(blocks):
            low, high = block(2 * p * blocks + j), block((2 * p + 1) * blocks + j)
            for a in range(STREAMS):
                for o in range(tensors):
                    part = slice(a * rows + 8 * o, a * rows + 8 * o + 8)
                    dst[a, p, o, :, 128 * j:128 * j + 128] = jnp.concatenate(
                        [low[part], high[part]], axis=0
                    ).astype(BF16)

    def wait_chunk(buffer, send, recv, a, p, src):
        remote(
            buffer.at[a, p, src], buffer.at[a, p, src], send.at[a, p, 0], recv.at[a, p, src], tensor=other(1)
        ).wait_recv()

    def wait_chunks(buffer, send, recv, a, p):
        for d in (0, *reversed(offsets)):
            wait_chunk(buffer, send, recv, a, p, other(d))

    def columns(p):
        return pl.ds(pl.multiple_of(p * span, span), span)

    def gated(buffer, a, ready):
        both[...] = jnp.zeros_like(both)
        square[...] = jnp.zeros_like(square)

        @pl.loop(0, PARTS)
        def _(p):
            ready(p)
            gain = gain_ref[:, columns(p)]
            squares = []
            for k in range(tensors // 2):
                pair = [unchunked(buffer[a, p, o]) for o in (2 * k, 2 * k + 1)]
                squares += [row_sum(v * v) for v in pair]
                normed[16 * k:16 * k + 16, columns(p)] = (jnp.concatenate(pair, axis=0) * gain).astype(BF16)
            square[...] += jnp.broadcast_to(jnp.concatenate(squares, axis=0), square.shape)
            both[...] += dot(normed[:, columns(p)], gate_up[columns(p), :])

        product = both[...] * lax.rsqrt(square[:, :1] / features + EPSILON)
        return product[:, :units], product[:, units:]

    def fill_q_rows(a, p):
        for k in range(tensors // 2):
            pair = [unchunked(qc[a, p, o]) for o in (2 * k, 2 * k + 1)]
            q_rows[a, 16 * k:16 * k + 16, columns(p)] = jnp.concatenate(pair, axis=0).astype(BF16)

    def back_product(a, ready):
        back[...] = jnp.zeros_like(back)

        @pl.loop(0, PARTS)
        def _(p):
            ready(p)
            fill_q_rows(a, p)
            back[...] += dot(q_rows[a, :, columns(p)], down_t[columns(p), :])

        return back[...]

    def fill(out, a, p, left, right):
        product[...] = dot(left, right[:, columns(p)])
        for o in range(tensors):
            out[a, p, o] = chunked(product[8 * o:8 * o + 8, :]).astype(BF16)

    def scatter_copies(out, land, send, recv, a, p):
        return [
            remote(
                out.at[a, p, other(d)], land.at[a, p, t], send.at[a, p, d], recv.at[a, p, t], tensor=other(d)
            )
            for d in offsets
        ]

    def scatter(out, land, send, recv, a, p):
        for copy in scatter_copies(out, land, send, recv, a, p):
            copy.start()

    def summed(out, land, send, recv, a, p):
        total = out[a, p, t].astype(F32)
        for d in reversed(offsets):
            wait_chunk(land, send, recv, a, p, other(d))
            total = total + land[a, p, other(d)].astype(F32)
        return total

    def spread_copies(src, dst, send, recv, a, p, section):
        return [
            remote(
                src.at[a, p], dst.at[a, p, t], send.at[a, p, d], recv.at[a, p, t], section=section,
                tensor=other(d),
            )
            for d in (*offsets, 0)
        ]

    def forward_copies(a, p):
        return spread_copies(f_sum, hc, fg_send, fg_recv, a, p, jnp.minimum(s + 1, last))

    def backward_copies(a, p):
        return spread_copies(b_sum, qc, bg_send, bg_recv, a, p, jnp.maximum(s - 1, 0))

    def own_copies(a, p):
        return spread_copies(b_sum, hn, own_send, own_recv, a, p, last)

    def relay_copy(a):
        return remote(f_out.at[a], b_out.at[a], relay_send.at[a], relay_recv.at[a], section=0, tensor=t)

    def rest_copy(a):
        return remote(hc.at[a, :, t], qc.at[a, :, t], rest_send.at[a], rest_recv.at[a], section=0, tensor=t)

    def send_back(a):
        return remote(
            hc.at[a], hn.at[a], back_send.at[a], back_recv.at[a], section=jnp.maximum(s - 1, 0), tensor=t
        )

    across = replicas // 2
    partner = lax.rem(r + across, replicas)

    def along(d):
        return (r // across) * across + lax.rem(r + d, across)

    def e_copies(a):
        return [
            remote(expanded.at[r, a], expanded.at[r, a], e_send.at[a, d], e_recv.at[a, r], dp=to)
            for d, to in enumerate([partner] + [along(d) for d in range(1, across)])
        ]

    def e_passed(a):
        return [
            remote(
                expanded.at[partner, a], expanded.at[partner, a], e_send.at[a, across + d],
                e_recv.at[a, partner], dp=along(d),
            )
            for d in range(1, across)
        ]

    def e_wait(a, src):
        remote(expanded.at[src, a], expanded.at[src, a], e_send.at[a, 0], e_recv.at[a, src], dp=partner).wait_recv()

    def send_expanded(a):
        for copy in e_copies(a):
            copy.start()

    def pass_expanded():
        @pl.loop(0, STREAMS)
        def _(a):
            e_wait(a, partner)
            for copy in e_passed(a):
                copy.start()

    def q_copy(d):
        width = q_cols.shape[-1]
        columns = pl.ds(pl.multiple_of(replica(d) * width, width), width)
        return remote(q_rows.at[:, :, columns], q_cols.at[r], q_send.at[d], q_recv.at[r], dp=replica(d))

    def send_q():
        width = q_cols.shape[-1]
        for d in range(1, replicas):
            q_copy(d).start()
        q_cols[r] = q_rows[:, :, pl.ds(pl.multiple_of(r * width, width), width)]

    def tail_copy(a, d):
        return remote(
            tail_out.at[a, replica(d)], tail_mid.at[a, r], t1_send.at[a, d], t1_recv.at[a, r], dp=replica(d)
        )

    def tail_spread(a):
        return [
            remote(
                tail_mid.at[a], tail_in.at[a, t], t2_send.at[a, d], t2_recv.at[a, t], section=0, tensor=other(d)
            )
            for d in (*offsets, 0)
        ]

    def owner_backward(a):
        grad = jnp.concatenate(
            [unchunked(summed(b_out, b_in, bs_send, bs_recv, a, p)) for p in range(PARTS)], axis=1
        )
        value = jnp.concatenate([unchunked(hc[a, p, t]) for p in range(PARTS)], axis=1)
        before = jnp.concatenate([unchunked(qc[a, p, t]) for p in range(PARTS)], axis=1)
        scale = lax.rsqrt(row_sum(value * value) / features + EPSILON)
        weighted = grad * gain_ref[...]
        pull = scale * scale * scale * (row_sum(value * weighted) / features)
        return before + scale * weighted - value * pull

    def backward_product(a, incoming):
        slopes[:, :units] = (incoming * gate_factor[a]).astype(BF16)
        slopes[:, units:] = (incoming * up_factor[a]).astype(BF16)
        @pl.loop(0, PARTS)
        def _(p):
            fill(b_out, a, p, slopes[...], gate_up_t)
            scatter(b_out, b_in, bs_send, bs_recv, a, p)

    def pass_back(a):
        row = owner_backward(a)
        for p in range(PARTS):
            b_sum[a, p] = chunked(row[:, p * span:(p + 1) * span]).astype(BF16)
            for copy in backward_copies(a, p):
                copy.start()

    def expand(a, ready):
        gate_new, up_new = gated(hn, a, ready)
        expanded[r, a] = (gate_new / (1.0 + jnp.exp(-gate_new)) * up_new).astype(BF16)

    def forward_sent():
        for which in (0, 1):
            each_piece(which, lambda copy: copy.wait_send())

        @pl.loop(0, STREAMS)
        def _(a):
            for copy in e_copies(a):
                copy.wait_send()

            @pl.when(s > 0)
            def _():
                send_back(a).wait_send()

            @pl.when(s < last)
            def _():
                for p in range(PARTS):
                    for copy in (*scatter_copies(f_out, f_in, fs_send, fs_recv, a, p), *forward_copies(a, p)):
                        copy.wait_send()

    def passed_sent():
        @pl.loop(0, STREAMS)
        def _(a):
            for copy in e_passed(a):
                copy.wait_send()

    def allow(section):
        pl.semaphore_signal(
            go, inc=1, device_id={"section": section, "tensor": t}, device_id_type=pl.DeviceIdType.MESH
        )

    for load in loads:
        load.wait()

    @pl.when(s > 0)
    def _():
        @pl.loop(0, features // 256)
        def _(j):
            part = pl.ds(pl.multiple_of(256 * j, 256), 256)
            down_t[part, :] = down[:, part].T
            gate_up_t[:, part] = gate_up[part, :].T

    @pl.when(s > 0)
    def _():
        each_piece(1, lambda copy: copy.start())

    @pl.when(s == last)
    def _():
        for p in range(PARTS):
            gather_pieces(1, qc, p)

        @pl.loop(0, STREAMS)
        def _(a):
            back_hidden[a] = back_product(a, lambda p: None)

        send_q()

    @pl.loop(0, STREAMS)
    def _(a):
        def ready(p):
            @pl.when(jnp.logical_and(s == 0, a == 0))
            def _():
                gather_pieces(0, hc, p)

            @pl.when(s > 0)
            def _():
                wait_chunks(hc, fg_send, fg_recv, a, p)

                @pl.when(p == PARTS - 1)
                def _():
                    send_back(a).start()

        gate_pre, up_pre = gated(hc, a, ready)
        sigmoid = 1.0 / (1.0 + jnp.exp(-gate_pre))
        silu = gate_pre * sigmoid
        hidden[a] = (silu * up_pre).astype(BF16)
        up_factor[a] = silu
        gate_factor[a] = up_pre * sigmoid * (1.0 + gate_pre * (1.0 - sigmoid))

        @pl.when(s < last)
        def _():
            @pl.loop(0, PARTS)
            def _(p):
                fill(f_out, a, p, hidden[a], down)
                scatter(f_out, f_in, fs_send, fs_recv, a, p)

        @pl.when(s == last)
        def _():
            backward_product(a, back_hidden[a])

    @pl.when(s == last)
    def _():
        @pl.loop(0, STREAMS)
        def _(a):
            @pl.loop(0, PARTS)
            def _(p):
                fill(f_out, a, p, hidden[a], down)

            for copy in (relay_copy(a), rest_copy(a)):
                copy.start()

    @pl.when(s < last)
    def _():
        @pl.loop(0, STREAMS)
        def _(a):
            @pl.loop(0, PARTS)
            def _(p):
                total = summed(f_out, f_in, fs_send, fs_recv, a, p)
                f_sum[a, p] = (hc[a, p, t].astype(F32) + total).astype(BF16)
                for copy in forward_copies(a, p):
                    copy.start()

        @pl.when(s == 0)
        def _():
            each_piece(1, lambda copy: copy.start())

        @pl.loop(0, STREAMS)
        def _(a):
            send_back(a).wait_recv()

            @pl.when(jnp.logical_and(s == 1, a == STREAMS - 1))
            def _():
                allow(0)

            expand(a, lambda p: None)

            @pl.when(s > 0)
            def _():
                send_expanded(a)

    @pl.when(s == 0)
    def _():
        pl.semaphore_wait(go, 1)

        @pl.loop(0, STREAMS)
        def _(a):
            send_expanded(a)

    @pl.when(s < 2)
    def _():
        pass_expanded()
        passed_sent()

    @pl.when(s < last)
    def _():
        forward_sent()

    @pl.when(s == 0)
    def _():
        @pl.loop(0, STREAMS)
        def _(a):
            relay_copy(a).wait_recv()
            for p in range(PARTS):
                scatter(b_out, b_in, bs_send, bs_recv, a, p)

        @pl.loop(0, STREAMS)
        def _(a):
            rest_copy(a).wait_recv()
            @pl.loop(0, PARTS)
            def _(p):
                total = summed(b_out, b_in, bs_send, bs_recv, a, p)
                b_sum[a, p] = (qc[a, p, t].astype(F32) + total).astype(BF16)
                for copy in own_copies(a, p):
                    copy.start()

        @pl.loop(0, STREAMS)
        def _(a):
            for p in range(PARTS):
                for copy in (*scatter_copies(b_out, b_in, bs_send, bs_recv, a, p), *own_copies(a, p)):
                    copy.wait_send()

    @pl.when(jnp.logical_and(s > 0, s < last))
    def _():
        @pl.loop(0, STREAMS)
        def _(a):
            backward_product(
                a, back_product(a, lambda p: wait_chunks(qc, bg_send, bg_recv, a, p))
            )

        send_q()

    @pl.when(s > 1)
    def _():
        @pl.loop(0, STREAMS)
        def _(a):
            pass_back(a)

    @pl.when(s == 2)
    def _():
        pass_expanded()

    @pl.when(s == 1)
    def _():
        @pl.loop(0, STREAMS)
        def _(a):
            row = owner_backward(a)
            width = q_cols.shape[-1]
            for k in range(replicas):
                tail_out[a, k] = chunked(row[:, k * width:(k + 1) * width]).astype(BF16)
            for d in range(1, replicas):
                tail_copy(a, d).start()
            tail_mid[a, r] = tail_out[a, r]

        @pl.loop(0, STREAMS)
        def _(a):
            for d in range(1, replicas):
                src = replica(d)
                remote(
                    tail_mid.at[a, src], tail_mid.at[a, src], t1_send.at[a, 0], t1_recv.at[a, src], dp=replica(1)
                ).wait_recv()
            for copy in tail_spread(a):
                copy.start()

    @pl.when(s == last)
    def _():
        @pl.loop(0, STREAMS)
        def _(a):
            expand(a, lambda p: wait_chunks(hn, own_send, own_recv, a, p))
            send_expanded(a)

        pass_expanded()

    @pl.when(s > 0)
    def _():
        for d in range(1, replicas):
            src = replica(d)
            remote(q_cols.at[src], q_cols.at[src], q_send.at[0], q_recv.at[src], dp=replica(1)).wait_recv()

    @pl.loop(0, STREAMS)
    def _(a):
        for d in range(1, replicas):
            if d != across:
                e_wait(a, replica(d))

    def gather_tail(a):
        for d in (0, *reversed(offsets)):
            src = other(d)
            remote(
                tail_in.at[a, src], tail_in.at[a, src], t2_send.at[a, 0], t2_recv.at[a, src], tensor=other(1)
            ).wait_recv()
        for k in range(replicas):
            for o in range(0, tensors, 2):
                group = [unchunked(tail_in[a, o + j, k]) for j in range(2)]
                q_cols[k, a, 8 * o:8 * o + 16, :] = jnp.concatenate(group, axis=0).astype(BF16)

    out_ref[...] = jnp.zeros_like(out_ref)

    @pl.loop(0, STREAMS)
    def _(a):
        @pl.when(s == 0)
        def _():
            gather_tail(a)

        every = replicas * rows
        out_ref[0] += lax.dot_general(
            expanded[:, a].reshape(every, units), q_cols[:, a].reshape(every, q_cols.shape[-1]),
            CONTRACT_FIRST, preferred_element_type=F32,
        )

    @pl.when(s == last)
    def _():
        forward_sent()

    @pl.when(s > 1)
    def _():
        passed_sent()

    @pl.when(s > 0)
    def _():
        for d in range(1, replicas):
            q_copy(d).wait_send()

        @pl.loop(0, STREAMS)
        def _(a):
            for p in range(PARTS):
                for copy in scatter_copies(b_out, b_in, bs_send, bs_recv, a, p):
                    copy.wait_send()

                @pl.when(s > 1)
                def _():
                    for copy in backward_copies(a, p):
                        copy.wait_send()

            @pl.when(s == last)
            def _():
                for copy in (relay_copy(a), rest_copy(a)):
                    copy.wait_send()

            @pl.when(s == 1)
            def _():
                for d in range(1, replicas):
                    tail_copy(a, d).wait_send()
                for copy in tail_spread(a):
                    copy.wait_send()


def solution(mesh):
    sections, tensors, replicas = (mesh.shape[name] for name in ("section", "tensor", "dp"))

    def shards(x_in, gate_weight, up_weight, down_weight, norm_gain, cotangent):
        features, units = gate_weight.shape[1:]
        rows = 8 * tensors
        width = features // replicas
        span = features // PARTS
        vmem, dma = pltpu.VMEM, pltpu.SemaphoreType.DMA
        chunks = vmem((STREAMS, PARTS, tensors, 16, span // 2), BF16)
        chunk = vmem((STREAMS, PARTS, 16, span // 2), BF16)
        factor = vmem((STREAMS, rows, units), F32)
        pair = [dma((STREAMS, PARTS, tensors))] * 2
        stream = [dma((STREAMS,))] * 2
        flat = [dma((STREAMS, tensors))] * 2
        local = pl.BlockSpec(memory_space=pltpu.VMEM)
        anywhere = pl.BlockSpec(memory_space=pl.ANY)
        return pl.pallas_call(
            functools.partial(kernel, (sections, tensors, replicas)),
            out_shape=vmem((1, units, width), F32),
            in_specs=[anywhere] * 6,
            out_specs=local,
            scratch_shapes=[
                vmem((1, features), F32),
                vmem((rows, 2 * units), F32),
                vmem((rows, units), F32),
                vmem((rows, 128), F32),
                vmem((features, 2 * units), BF16),
                vmem((units, features), BF16),
                vmem((features, units), BF16),
                vmem((2 * units, features), BF16),
                vmem((sections * tensors, *x_in.shape[:0:-1]), BF16),
                chunks, chunks, chunks,
                vmem((rows, features), BF16),
                vmem((rows, span), F32),
                vmem((STREAMS, rows, units), BF16),
                vmem((rows, 2 * units), BF16),
                factor, factor, factor,
                chunks, chunks, chunks, chunks,
                chunk, chunk,
                vmem((STREAMS, replicas, 16, width // 2), BF16),
                vmem((STREAMS, replicas, 16, width // 2), BF16),
                vmem((STREAMS, tensors, replicas, 16, width // 2), BF16),
                vmem((STREAMS, rows, features), BF16),
                vmem((replicas, STREAMS, rows, width), BF16),
                vmem((replicas, STREAMS, rows, units), BF16),
                dma((4,)),
                dma((2, tensors)), dma((sections * tensors,)),
                *pair, *pair, *pair, *pair,
                *stream,
                *pair,
                *stream, *stream,
                dma((STREAMS, replicas)), dma((STREAMS, replicas)),
                dma((replicas,)), dma((replicas,)),
                dma((STREAMS, replicas)), dma((STREAMS, replicas)),
                *flat,
                pltpu.SemaphoreType.REGULAR,
            ],
            compiler_params=pltpu.CompilerParams(
                collective_id=0, has_side_effects=True, vmem_limit_bytes=56 * 1024 * 1024
            ),
            name="expanded_step",
        )(jnp.swapaxes(x_in, 1, 2), jnp.swapaxes(cotangent, 1, 2), norm_gain, gate_weight, up_weight, down_weight)

    placed = (
        P(None, "dp", ("section", "tensor")),
        P("section", None, "tensor"),
        P("section", None, "tensor"),
        P("section", "tensor", None),
        P("section", None),
        P(None, "dp", ("section", "tensor")),
    )
    return jax.shard_map(
        shards, mesh=mesh, in_specs=placed, out_specs=P("section", "tensor", "dp"), check_vma=False
    )
```

```python
import functools

import jax
import jax.numpy as jnp
from jax import lax
from jax.experimental import pallas as pl
from jax.experimental.pallas import tpu as pltpu
from jax.sharding import PartitionSpec as P

EPSILON = 1e-05
F32, BF16 = jnp.float32, jnp.bfloat16
CONTRACT_FIRST = (((0,), (0,)), ((), ()))
STREAMS = 2
PARTS = 2


def dot(left, right):
    return jnp.dot(left, right, preferred_element_type=F32)


def chunked(rows):
    half = rows.shape[1] // 2
    return jnp.concatenate([rows[:, :half], rows[:, half:]], axis=0)


def unchunked(chunk):
    chunk = chunk.astype(F32)
    return jnp.concatenate([chunk[:8], chunk[8:]], axis=1)


def row_sum(values):
    return jnp.sum(values, axis=-1, keepdims=True)


def kernel(
    sizes, x_ref, c_ref, gain_hbm, gate_hbm, up_hbm, down_hbm, out_ref,
    gain_ref, both, back, square, gate_up, down, down_t, gate_up_t, landing, hc, hn, qc, normed, product, hidden, slopes,
    gate_factor, up_factor, back_hidden, f_out, f_in, b_out, b_in, f_sum, b_sum, tail_out, tail_mid,
    tail_in, q_rows, q_cols, expanded,
    w_sem, piece_send, piece_recv, fs_send, fs_recv, bs_send, bs_recv, fg_send, fg_recv, bg_send, bg_recv,
    back_send, back_recv, own_send, own_recv, relay_send, relay_recv, rest_send, rest_recv, e_send, e_recv,
    q_send, q_recv, t1_send, t1_recv, t2_send, t2_recv, go,
):
    sections, tensors, replicas = sizes
    s, t, r = lax.axis_index("section"), lax.axis_index("tensor"), lax.axis_index("dp")
    last = sections - 1
    features = down.shape[1]
    span = features // PARTS
    units = down.shape[0]
    rows = normed.shape[0]
    offsets = sorted(range(1, tensors), key=lambda d: (-min(d, tensors - d), d))
    me = s * tensors + t

    def remote(src, dst, send, recv, **where):
        return pltpu.make_async_remote_copy(
            src_ref=src, dst_ref=dst, send_sem=send, recv_sem=recv, device_id=where,
            device_id_type=pl.DeviceIdType.MESH,
        )

    def other(d):
        return lax.rem(t + d, tensors)

    def replica(d):
        return lax.rem(r + d, replicas)

    loads = [
        pltpu.make_async_copy(src, dst, w_sem.at[i])
        for i, (src, dst) in enumerate((
            (gain_hbm, gain_ref), (gate_hbm.at[0], gate_up.at[:, :units]), (up_hbm.at[0], gate_up.at[:, units:]),
            (down_hbm.at[0], down),
        ))
    ]
    for load in loads:
        load.start()

    barrier = pltpu.get_barrier_semaphore()
    for d in (*offsets, 0):
        for k in range(sections):
            if d or k:
                pl.semaphore_signal(
                    barrier, inc=1, device_id={"section": lax.rem(s + k, sections), "tensor": other(d)},
                    device_id_type=pl.DeviceIdType.MESH,
                )
        if d == offsets[0]:
            for k in range(1, replicas):
                pl.semaphore_signal(
                    barrier, inc=1, device_id={"dp": replica(k)}, device_id_type=pl.DeviceIdType.MESH
                )
    pl.semaphore_wait(barrier, sections * tensors + replicas - 2)

    inputs = (x_ref, c_ref)

    def piece_copy(which, d):
        return remote(
            inputs[which].at[0], landing.at[me], piece_send.at[which, d], piece_recv.at[me],
            section=0 if which == 0 else last, tensor=other(d),
        )

    def each_piece(which, action):
        home = 0 if which == 0 else last
        for d in offsets:
            action(piece_copy(which, d))

        @pl.when(s != home)
        def _():
            action(piece_copy(which, 0))

    each_piece(0, lambda copy: copy.start())

    def own_piece(which):
        return pltpu.make_async_copy(inputs[which].at[0], landing.at[me], piece_recv.at[me])

    @pl.when(s == 0)
    def _():
        own_piece(0).start()

    @pl.when(s == last)
    def _():
        own_piece(1).start()

    def gather_pieces(which, dst, p):
        count = sections * tensors // PARTS

        @pl.loop(p * count, (p + 1) * count)
        def _(src):
            @pl.when(src == me)
            def _():
                own_piece(which).wait()

            @pl.when(src != me)
            def _():
                remote(
                    inputs[which].at[0], landing.at[src], piece_send.at[which, 0], piece_recv.at[src],
                    tensor=other(1),
                ).wait_recv()

        def block(j):
            return jnp.concatenate([landing[2 * j].astype(F32), landing[2 * j + 1].astype(F32)], axis=0).T

        blocks = span // 256
        for j in range(blocks):
            low, high = block(2 * p * blocks + j), block((2 * p + 1) * blocks + j)
            for a in range(STREAMS):
                for o in range(tensors):
                    part = slice(a * rows + 8 * o, a * rows + 8 * o + 8)
                    dst[a, p, o, :, 128 * j:128 * j + 128] = jnp.concatenate(
                        [low[part], high[part]], axis=0
                    ).astype(BF16)

    def wait_chunk(buffer, send, recv, a, p, src):
        remote(
            buffer.at[a, p, src], buffer.at[a, p, src], send.at[a, p, 0], recv.at[a, p, src], tensor=other(1)
        ).wait_recv()

    def wait_chunks(buffer, send, recv, a, p):
        for d in (0, *reversed(offsets)):
            wait_chunk(buffer, send, recv, a, p, other(d))

    def columns(p):
        return pl.ds(pl.multiple_of(p * span, span), span)

    def gated(buffer, a, ready):
        both[...] = jnp.zeros_like(both)
        square[...] = jnp.zeros_like(square)

        @pl.loop(0, PARTS)
        def _(p):
            ready(p)
            gain = gain_ref[:, columns(p)]
            squares = []
            for k in range(tensors // 2):
                pair = [unchunked(buffer[a, p, o]) for o in (2 * k, 2 * k + 1)]
                squares += [row_sum(v * v) for v in pair]
                normed[16 * k:16 * k + 16, columns(p)] = (jnp.concatenate(pair, axis=0) * gain).astype(BF16)
            square[...] += jnp.broadcast_to(jnp.concatenate(squares, axis=0), square.shape)
            both[...] += dot(normed[:, columns(p)], gate_up[columns(p), :])

        product = both[...] * lax.rsqrt(square[:, :1] / features + EPSILON)
        return product[:, :units], product[:, units:]

    def fill_q_rows(a, p):
        for k in range(tensors // 2):
            pair = [unchunked(qc[a, p, o]) for o in (2 * k, 2 * k + 1)]
            q_rows[a, 16 * k:16 * k + 16, columns(p)] = jnp.concatenate(pair, axis=0).astype(BF16)

    def back_product(a, ready):
        back[...] = jnp.zeros_like(back)

        @pl.loop(0, PARTS)
        def _(p):
            ready(p)
            fill_q_rows(a, p)
            back[...] += dot(q_rows[a, :, columns(p)], down_t[columns(p), :])

        return back[...]

    def fill(out, a, p, left, right):
        product[...] = dot(left, right[:, columns(p)])
        for o in range(tensors):
            out[a, p, o] = chunked(product[8 * o:8 * o + 8, :]).astype(BF16)

    def scatter_copies(out, land, send, recv, a, p):
        return [
            remote(
                out.at[a, p, other(d)], land.at[a, p, t], send.at[a, p, d], recv.at[a, p, t], tensor=other(d)
            )
            for d in offsets
        ]

    def scatter(out, land, send, recv, a, p):
        for copy in scatter_copies(out, land, send, recv, a, p):
            copy.start()

    def summed(out, land, send, recv, a, p):
        total = out[a, p, t].astype(F32)
        for d in reversed(offsets):
            wait_chunk(land, send, recv, a, p, other(d))
            total = total + land[a, p, other(d)].astype(F32)
        return total

    def spread_copies(src, dst, send, recv, a, p, section):
        return [
            remote(
                src.at[a, p], dst.at[a, p, t], send.at[a, p, d], recv.at[a, p, t], section=section,
                tensor=other(d),
            )
            for d in (*offsets, 0)
        ]

    def forward_copies(a, p):
        return spread_copies(f_sum, hc, fg_send, fg_recv, a, p, jnp.minimum(s + 1, last))

    def backward_copies(a, p):
        return spread_copies(b_sum, qc, bg_send, bg_recv, a, p, jnp.maximum(s - 1, 0))

    def own_copies(a, p):
        return spread_copies(b_sum, hn, own_send, own_recv, a, p, last)

    def relay_copy(a):
        return remote(f_out.at[a], b_out.at[a], relay_send.at[a], relay_recv.at[a], section=0, tensor=t)

    def rest_copy(a):
        return remote(hc.at[a, :, t], qc.at[a, :, t], rest_send.at[a], rest_recv.at[a], section=0, tensor=t)

    def send_back(a):
        return remote(
            hc.at[a], hn.at[a], back_send.at[a], back_recv.at[a], section=jnp.maximum(s - 1, 0), tensor=t
        )

    across = replicas // 2
    partner = lax.rem(r + across, replicas)

    def along(d):
        return (r // across) * across + lax.rem(r + d, across)

    def e_copies(a):
        return [
            remote(expanded.at[r, a], expanded.at[r, a], e_send.at[a, d], e_recv.at[a, r], dp=to)
            for d, to in enumerate([partner] + [along(d) for d in range(1, across)])
        ]

    def e_passed(a):
        return [
            remote(
                expanded.at[partner, a], expanded.at[partner, a], e_send.at[a, across + d],
                e_recv.at[a, partner], dp=along(d),
            )
            for d in range(1, across)
        ]

    def e_wait(a, src):
        remote(expanded.at[src, a], expanded.at[src, a], e_send.at[a, 0], e_recv.at[a, src], dp=partner).wait_recv()

    def send_expanded(a):
        for copy in e_copies(a):
            copy.start()

    def pass_expanded():
        @pl.loop(0, STREAMS)
        def _(a):
            e_wait(a, partner)
            for copy in e_passed(a):
                copy.start()

    def q_copy(a, d):
        width = q_cols.shape[-1]
        part = pl.ds(pl.multiple_of(replica(d) * width, width), width)
        return remote(q_rows.at[a, :, part], q_cols.at[r, a], q_send.at[a, d], q_recv.at[a, r], dp=replica(d))

    def send_q(a):
        width = q_cols.shape[-1]
        for d in range(1, replicas):
            q_copy(a, d).start()
        q_cols[r, a] = q_rows[a, :, pl.ds(pl.multiple_of(r * width, width), width)]

    def tail_copy(a, d):
        return remote(
            tail_out.at[a, replica(d)], tail_mid.at[a, r], t1_send.at[a, d], t1_recv.at[a, r], dp=replica(d)
        )

    def tail_spread(a):
        return [
            remote(
                tail_mid.at[a], tail_in.at[a, t], t2_send.at[a, d], t2_recv.at[a, t], section=0, tensor=other(d)
            )
            for d in (*offsets, 0)
        ]

    def owner_backward(a):
        grad = jnp.concatenate(
            [unchunked(summed(b_out, b_in, bs_send, bs_recv, a, p)) for p in range(PARTS)], axis=1
        )
        value = jnp.concatenate([unchunked(hc[a, p, t]) for p in range(PARTS)], axis=1)
        before = jnp.concatenate([unchunked(qc[a, p, t]) for p in range(PARTS)], axis=1)
        scale = lax.rsqrt(row_sum(value * value) / features + EPSILON)
        weighted = grad * gain_ref[...]
        pull = scale * scale * scale * (row_sum(value * weighted) / features)
        return before + scale * weighted - value * pull

    def backward_product(a, incoming):
        slopes[:, :units] = (incoming * gate_factor[a]).astype(BF16)
        slopes[:, units:] = (incoming * up_factor[a]).astype(BF16)
        @pl.loop(0, PARTS)
        def _(p):
            fill(b_out, a, p, slopes[...], gate_up_t)
            scatter(b_out, b_in, bs_send, bs_recv, a, p)

    def pass_back(a):
        row = owner_backward(a)
        for p in range(PARTS):
            b_sum[a, p] = chunked(row[:, p * span:(p + 1) * span]).astype(BF16)
            for copy in backward_copies(a, p):
                copy.start()

    def expand(a, ready):
        gate_new, up_new = gated(hn, a, ready)
        expanded[r, a] = (gate_new / (1.0 + jnp.exp(-gate_new)) * up_new).astype(BF16)

    def forward_sent():
        for which in (0, 1):
            each_piece(which, lambda copy: copy.wait_send())

        @pl.loop(0, STREAMS)
        def _(a):
            for copy in e_copies(a):
                copy.wait_send()

            @pl.when(s > 0)
            def _():
                send_back(a).wait_send()

            @pl.when(s < last)
            def _():
                for p in range(PARTS):
                    for copy in (*scatter_copies(f_out, f_in, fs_send, fs_recv, a, p), *forward_copies(a, p)):
                        copy.wait_send()

    def passed_sent():
        @pl.loop(0, STREAMS)
        def _(a):
            for copy in e_passed(a):
                copy.wait_send()

    def allow(section):
        pl.semaphore_signal(
            go, inc=1, device_id={"section": section, "tensor": t}, device_id_type=pl.DeviceIdType.MESH
        )

    for load in loads:
        load.wait()

    @pl.when(s > 0)
    def _():
        @pl.loop(0, features // 256)
        def _(j):
            part = pl.ds(pl.multiple_of(256 * j, 256), 256)
            down_t[part, :] = down[:, part].T
            gate_up_t[:, part] = gate_up[part, :].T

    @pl.when(s > 0)
    def _():
        each_piece(1, lambda copy: copy.start())

    @pl.when(s == last)
    def _():
        for p in range(PARTS):
            gather_pieces(1, qc, p)

        @pl.loop(0, STREAMS)
        def _(a):
            back_hidden[a] = back_product(a, lambda p: None)
            send_q(a)

    @pl.loop(0, STREAMS)
    def _(a):
        def ready(p):
            @pl.when(jnp.logical_and(s == 0, a == 0))
            def _():
                gather_pieces(0, hc, p)

            @pl.when(s > 0)
            def _():
                wait_chunks(hc, fg_send, fg_recv, a, p)

                @pl.when(p == PARTS - 1)
                def _():
                    send_back(a).start()

        gate_pre, up_pre = gated(hc, a, ready)
        sigmoid = 1.0 / (1.0 + jnp.exp(-gate_pre))
        silu = gate_pre * sigmoid
        hidden[a] = (silu * up_pre).astype(BF16)
        up_factor[a] = silu
        gate_factor[a] = up_pre * sigmoid * (1.0 + gate_pre * (1.0 - sigmoid))

        @pl.when(s < last)
        def _():
            @pl.loop(0, PARTS)
            def _(p):
                fill(f_out, a, p, hidden[a], down)
                scatter(f_out, f_in, fs_send, fs_recv, a, p)

        @pl.when(s == last)
        def _():
            backward_product(a, back_hidden[a])

    @pl.when(s == last)
    def _():
        @pl.loop(0, STREAMS)
        def _(a):
            @pl.loop(0, PARTS)
            def _(p):
                fill(f_out, a, p, hidden[a], down)

            for copy in (relay_copy(a), rest_copy(a)):
                copy.start()

    @pl.when(s < last)
    def _():
        @pl.loop(0, STREAMS)
        def _(a):
            @pl.loop(0, PARTS)
            def _(p):
                total = summed(f_out, f_in, fs_send, fs_recv, a, p)
                f_sum[a, p] = (hc[a, p, t].astype(F32) + total).astype(BF16)
                for copy in forward_copies(a, p):
                    copy.start()

        @pl.when(s == 0)
        def _():
            each_piece(1, lambda copy: copy.start())

        @pl.loop(0, STREAMS)
        def _(a):
            send_back(a).wait_recv()

            @pl.when(jnp.logical_and(s == 1, a == STREAMS - 1))
            def _():
                allow(0)

            expand(a, lambda p: None)

            @pl.when(s > 0)
            def _():
                send_expanded(a)

    @pl.when(s == 0)
    def _():
        pl.semaphore_wait(go, 1)

        @pl.loop(0, STREAMS)
        def _(a):
            send_expanded(a)

    @pl.when(s < 2)
    def _():
        pass_expanded()
        passed_sent()

    @pl.when(s < last)
    def _():
        forward_sent()

    @pl.when(s == 0)
    def _():
        @pl.loop(0, STREAMS)
        def _(a):
            relay_copy(a).wait_recv()
            for p in range(PARTS):
                scatter(b_out, b_in, bs_send, bs_recv, a, p)

        @pl.loop(0, STREAMS)
        def _(a):
            rest_copy(a).wait_recv()
            @pl.loop(0, PARTS)
            def _(p):
                total = summed(b_out, b_in, bs_send, bs_recv, a, p)
                b_sum[a, p] = (qc[a, p, t].astype(F32) + total).astype(BF16)
                for copy in own_copies(a, p):
                    copy.start()

        @pl.loop(0, STREAMS)
        def _(a):
            for p in range(PARTS):
                for copy in (*scatter_copies(b_out, b_in, bs_send, bs_recv, a, p), *own_copies(a, p)):
                    copy.wait_send()

    @pl.when(jnp.logical_and(s > 0, s < last))
    def _():
        @pl.loop(0, STREAMS)
        def _(a):
            incoming = back_product(a, lambda p: wait_chunks(qc, bg_send, bg_recv, a, p))
            send_q(a)
            backward_product(a, incoming)

    @pl.when(s > 1)
    def _():
        @pl.loop(0, STREAMS)
        def _(a):
            pass_back(a)

    @pl.when(s == 2)
    def _():
        pass_expanded()

    @pl.when(s == 1)
    def _():
        @pl.loop(0, STREAMS)
        def _(a):
            row = owner_backward(a)
            width = q_cols.shape[-1]
            for k in range(replicas):
                tail_out[a, k] = chunked(row[:, k * width:(k + 1) * width]).astype(BF16)
            for d in range(1, replicas):
                tail_copy(a, d).start()
            tail_mid[a, r] = tail_out[a, r]

        @pl.loop(0, STREAMS)
        def _(a):
            for d in range(1, replicas):
                src = replica(d)
                remote(
                    tail_mid.at[a, src], tail_mid.at[a, src], t1_send.at[a, 0], t1_recv.at[a, src], dp=replica(1)
                ).wait_recv()
            for copy in tail_spread(a):
                copy.start()

    @pl.when(s == last)
    def _():
        @pl.loop(0, STREAMS)
        def _(a):
            expand(a, lambda p: wait_chunks(hn, own_send, own_recv, a, p))
            send_expanded(a)

        pass_expanded()

    @pl.when(s > 0)
    def _():
        @pl.loop(0, STREAMS)
        def _(a):
            for d in range(1, replicas):
                src = replica(d)
                remote(
                    q_cols.at[src, a], q_cols.at[src, a], q_send.at[a, 0], q_recv.at[a, src], dp=replica(1)
                ).wait_recv()

    @pl.loop(0, STREAMS)
    def _(a):
        for d in range(1, replicas):
            if d != across:
                e_wait(a, replica(d))

    def gather_tail(a):
        for d in (0, *reversed(offsets)):
            src = other(d)
            remote(
                tail_in.at[a, src], tail_in.at[a, src], t2_send.at[a, 0], t2_recv.at[a, src], tensor=other(1)
            ).wait_recv()
        for k in range(replicas):
            for o in range(0, tensors, 2):
                group = [unchunked(tail_in[a, o + j, k]) for j in range(2)]
                q_cols[k, a, 8 * o:8 * o + 16, :] = jnp.concatenate(group, axis=0).astype(BF16)

    out_ref[...] = jnp.zeros_like(out_ref)

    @pl.loop(0, STREAMS)
    def _(a):
        @pl.when(s == 0)
        def _():
            gather_tail(a)

        every = replicas * rows
        out_ref[0] += lax.dot_general(
            expanded[:, a].reshape(every, units), q_cols[:, a].reshape(every, q_cols.shape[-1]),
            CONTRACT_FIRST, preferred_element_type=F32,
        )

    @pl.when(s == last)
    def _():
        forward_sent()

    @pl.when(s > 1)
    def _():
        passed_sent()

    @pl.when(s > 0)
    def _():
        @pl.loop(0, STREAMS)
        def _(a):
            for d in range(1, replicas):
                q_copy(a, d).wait_send()

            for p in range(PARTS):
                for copy in scatter_copies(b_out, b_in, bs_send, bs_recv, a, p):
                    copy.wait_send()

                @pl.when(s > 1)
                def _():
                    for copy in backward_copies(a, p):
                        copy.wait_send()

            @pl.when(s == last)
            def _():
                for copy in (relay_copy(a), rest_copy(a)):
                    copy.wait_send()

            @pl.when(s == 1)
            def _():
                for d in range(1, replicas):
                    tail_copy(a, d).wait_send()
                for copy in tail_spread(a):
                    copy.wait_send()


def solution(mesh):
    sections, tensors, replicas = (mesh.shape[name] for name in ("section", "tensor", "dp"))

    def shards(x_in, gate_weight, up_weight, down_weight, norm_gain, cotangent):
        features, units = gate_weight.shape[1:]
        rows = 8 * tensors
        width = features // replicas
        span = features // PARTS
        vmem, dma = pltpu.VMEM, pltpu.SemaphoreType.DMA
        chunks = vmem((STREAMS, PARTS, tensors, 16, span // 2), BF16)
        chunk = vmem((STREAMS, PARTS, 16, span // 2), BF16)
        factor = vmem((STREAMS, rows, units), F32)
        pair = [dma((STREAMS, PARTS, tensors))] * 2
        stream = [dma((STREAMS,))] * 2
        flat = [dma((STREAMS, tensors))] * 2
        local = pl.BlockSpec(memory_space=pltpu.VMEM)
        anywhere = pl.BlockSpec(memory_space=pl.ANY)
        return pl.pallas_call(
            functools.partial(kernel, (sections, tensors, replicas)),
            out_shape=vmem((1, units, width), F32),
            in_specs=[anywhere] * 6,
            out_specs=local,
            scratch_shapes=[
                vmem((1, features), F32),
                vmem((rows, 2 * units), F32),
                vmem((rows, units), F32),
                vmem((rows, 128), F32),
                vmem((features, 2 * units), BF16),
                vmem((units, features), BF16),
                vmem((features, units), BF16),
                vmem((2 * units, features), BF16),
                vmem((sections * tensors, *x_in.shape[:0:-1]), BF16),
                chunks, chunks, chunks,
                vmem((rows, features), BF16),
                vmem((rows, span), F32),
                vmem((STREAMS, rows, units), BF16),
                vmem((rows, 2 * units), BF16),
                factor, factor, factor,
                chunks, chunks, chunks, chunks,
                chunk, chunk,
                vmem((STREAMS, replicas, 16, width // 2), BF16),
                vmem((STREAMS, replicas, 16, width // 2), BF16),
                vmem((STREAMS, tensors, replicas, 16, width // 2), BF16),
                vmem((STREAMS, rows, features), BF16),
                vmem((replicas, STREAMS, rows, width), BF16),
                vmem((replicas, STREAMS, rows, units), BF16),
                dma((4,)),
                dma((2, tensors)), dma((sections * tensors,)),
                *pair, *pair, *pair, *pair,
                *stream,
                *pair,
                *stream, *stream,
                dma((STREAMS, replicas)), dma((STREAMS, replicas)),
                dma((STREAMS, replicas)), dma((STREAMS, replicas)),
                dma((STREAMS, replicas)), dma((STREAMS, replicas)),
                *flat,
                pltpu.SemaphoreType.REGULAR,
            ],
            compiler_params=pltpu.CompilerParams(
                collective_id=0, has_side_effects=True, vmem_limit_bytes=56 * 1024 * 1024
            ),
            name="expanded_step",
        )(jnp.swapaxes(x_in, 1, 2), jnp.swapaxes(cotangent, 1, 2), norm_gain, gate_weight, up_weight, down_weight)

    placed = (
        P(None, "dp", ("section", "tensor")),
        P("section", None, "tensor"),
        P("section", None, "tensor"),
        P("section", "tensor", None),
        P("section", None),
        P(None, "dp", ("section", "tensor")),
    )
    return jax.shard_map(
        shards, mesh=mesh, in_specs=placed, out_specs=P("section", "tensor", "dp"), check_vma=False
    )
```
